128 devices in a mesh: expert: 64 (over z, x, y), mp: 2 (over core).
Axes of the slice: x: 4, y: 4, z: 4, core: 2. Of those that a mesh axis runs over, the one named last changes fastest.
Arguments:
- tokens: bfloat16 [4096, 3584], P('expert', 'mp'), may hold values from -6 to 6
- cotangent: bfloat16 [4096, 3584], P('expert', 'mp'), may hold values from -6 to 6
- route_ids: int32 [4096, 8], P('expert'), may hold values from 0 to 63, all different within a row; in each aligned block of 64 rows (0 to 63, 64 to 127, ...) at most 12 rows name the same one
- gate_probs: float32 [4096, 8], P('expert'), may hold values from 0.02 to 0.5
- w_gate: bfloat16 [64, 3584, 1024], P('expert', None, 'mp'), may hold values from -0.09375 to 0.09375
- w_up: bfloat16 [64, 3584, 1024], P('expert', None, 'mp'), may hold values from -0.09375 to 0.09375
- w_down: bfloat16 [64, 1024, 3584], P('expert', 'mp'), may hold values from -0.1875 to 0.1875
Outputs:
- layer_out: bfloat16 [4096, 3584], P('expert', 'mp')
- grad_tokens: bfloat16 [4096, 3584], P('expert', 'mp')
- grad_probs: float32 [4096, 8], P('expert')
- grad_w_gate: bfloat16 [64, 3584, 1024], P('expert', None, 'mp')
- grad_w_up: bfloat16 [64, 3584, 1024], P('expert', None, 'mp')
- grad_w_down: bfloat16 [64, 1024, 3584], P('expert', 'mp')
The draws below stay inside these ranges and needn't reach their ends.
Inputs may be any that keep to these rules, and one draw needn't show every extreme that they name: `route_ids`: each token names 8 different experts. Within the tokens of one device (aligned blocks of 64 tokens) no expert is named more than 12 times, and in some block one expert is named exactly 12 times.
All inputs are finite; a program needn't handle non-finite values.
Results may differ from the reference program's by a relative error of at most 0.015.
Values may be sent and summed in bfloat16 or wider, within the bound.
No kernel may reach another device: no remote copies, remote signals or barrier semaphores. Data moves between devices by JAX's collectives and lax.ppermute only.
A program may use at most 192 MiB of HBM per device.

```python
import math
import jax
import jax.numpy as jnp
import numpy as np
from jax import lax

D = 3584
FF = 1024
TOPK = 8
TOK_DEV = 64
EXPERTS = 64
MOST = 12
TOKENS = 4096
N_EXPERT = 64


def block_levels(own_key, dims, pieces, low, largest):
    level, own = 1.0, jax.random.fold_in(own_key, 6)
    for position, parts in pieces:
        steps = jnp.exp(jax.random.uniform(jax.random.fold_in(own, position), (parts,), jnp.float32, low / len(pieces), largest / len(pieces)))
        level = level * jnp.repeat(steps, dims[position] // parts).reshape([-1 if axis == position else 1 for axis in range(len(dims))])
    return level


def shared_out(own_key, own, number, rows, number_of, top, limit, lean):
    ranking = jax.random.permutation(own_key, number_of)
    heavy_load, common = portions_of(number_of, rows * top, limit, lean, True), portions_of(number_of, rows * top, limit, lean, False)
    places = jnp.arange(number_of)

    def named(sizes, offset_by):
        used = int((sizes > 0).sum())
        fixed = max(1, used // 4)
        moved = fixed + (places - fixed + offset_by * (used - fixed)) % max(1, number_of - fixed)
        return jnp.zeros((number_of,), jnp.int32).at[ranking[jnp.where(places < fixed, places, moved)]].set(jnp.asarray(sizes, jnp.int32))

    sizes = jnp.where(number % 4 == 0, named(heavy_load, number // 4), named(common, number - number // 4 - 1))
    mixed = jax.random.permutation(jax.random.fold_in(own, 3), number_of)
    giver, receiver = mixed[0:number_of // 2 * 2:2], mixed[1:number_of // 2 * 2:2]
    margin = jnp.minimum(sizes[giver] - 1, limit - sizes[receiver]) // 2
    margin = jnp.where((giver == ranking[0]) | (receiver == ranking[0]) | (sizes[receiver] == 0), 0, jnp.maximum(margin, 0))
    moved = jax.random.randint(jax.random.fold_in(own, 4), (number_of // 2,), 0, 1 << 20) % (margin + 1)
    sizes = sizes.at[giver].add(-moved).at[receiver].add(moved)
    labels = jnp.searchsorted(jnp.cumsum(sizes), jnp.arange(rows * top), side="right").astype(jnp.int32)
    listing = labels.reshape(top, rows).T
    listing = listing[jax.random.permutation(jax.random.fold_in(own, 1), rows)]
    offset_by = jax.random.randint(jax.random.fold_in(own, 2), (rows, 1), 0, top)
    return jnp.take_along_axis(listing, (jnp.arange(top)[None, :] + offset_by) % top, axis=1)


def portions_of(number_of, total, reach, lean, full):
    loads = [(1 << 20) // math.isqrt(rank ** lean) + 1 for rank in range(1, number_of + 1)]
    largest = reach if full else min(reach, max(-(-total // number_of), total * loads[0] // sum(loads)))
    least = 1 if total - largest >= number_of - 1 else 0
    holding, spare = [largest] + [least] * (number_of - 1), total - largest - least * (number_of - 1)
    while spare > 0:
        candidates = [i for i in range(1, number_of) if holding[i] < largest] or [i for i in range(1, number_of) if holding[i] < reach]
        whole, remaining = sum([loads[i] for i in candidates]), spare
        for i in candidates:
            more = min(reach - holding[i], max(1, remaining * loads[i] // whole), spare)
            holding[i] = holding[i] + more
            spare = spare - more
    return np.array(holding)


def bell_draw(own_key, shape, deviation, most, cuts=(), held_as=jnp.bfloat16):
    values = deviation * jax.random.normal(own_key, shape, jnp.float32)
    if cuts:
        values = values * block_levels(own_key, shape, cuts, -0.22, 0.18)
    return jnp.clip(values, -most, most).astype(held_as)


def setup_inputs(seed: int = 0) -> dict:
    seeds = jax.random.split(jax.random.key(seed), 8)
    tokens = bell_draw(seeds[0], (TOKENS, D), 1.0, 6.0, ((0, 64), (1, 2)))
    cotangent = bell_draw(seeds[1], (TOKENS, D), 1.0, 6.0, ((0, 64), (1, 2)))
    route_ids_keys = jax.random.split(jax.random.fold_in(seeds[2], 1), TOKENS // TOK_DEV)
    route_ids_turns = jax.random.permutation(jax.random.fold_in(seeds[2], 3), TOKENS // TOK_DEV)
    route_ids = jax.vmap(lambda own, number: shared_out(jax.random.fold_in(seeds[2], 2), own, number, TOK_DEV, EXPERTS, TOPK, MOST, 2))(route_ids_keys, route_ids_turns).reshape((TOKENS, TOPK))
    gate_probs = jnp.clip(jnp.exp(math.log(0.5) - 3.218876 * jax.random.uniform(seeds[3], (TOKENS, TOPK), jnp.float32) ** block_levels(seeds[3], (TOKENS, TOPK), ((0, 64),), -0.2, 0.2)), 0.02, 0.5)
    w_gate = bell_draw(seeds[4], (EXPERTS, D, FF), D ** -0.5, 0.09375, ((0, 64), (2, 2)))
    w_up = bell_draw(seeds[5], (EXPERTS, D, FF), D ** -0.5, 0.09375, ((0, 64), (2, 2)))
    w_down = bell_draw(seeds[6], (EXPERTS, FF, D), FF ** -0.5, 0.1875, ((0, 64), (1, 2)))
    return {"tokens": tokens, "cotangent": cotangent, "route_ids": route_ids, "gate_probs": gate_probs, "w_gate": w_gate, "w_up": w_up, "w_down": w_down}


def reference(tokens, cotangent, route_ids, gate_probs, w_gate, w_up, w_down):
    assigns = TOKENS * TOPK
    capacity = N_EXPERT * MOST
    flat_ids = route_ids.reshape(-1).astype(jnp.int32)
    onehot = (flat_ids[:, None] == jnp.arange(EXPERTS, dtype=jnp.int32)[None, :]).astype(jnp.int32)
    blocked = onehot.reshape(N_EXPERT, TOK_DEV * TOPK, EXPERTS)
    earlier = jnp.cumsum(blocked, axis=1) - blocked
    slot_of = jnp.sum(earlier * blocked, axis=2).reshape(-1).astype(jnp.int32)
    source = (jnp.arange(assigns, dtype=jnp.int32) // (TOK_DEV * TOPK)).astype(jnp.int32)
    row_in = (source * MOST + slot_of).astype(jnp.int32)
    row_table = jnp.full((EXPERTS, capacity), assigns, dtype=jnp.int32)
    row_table = row_table.at[flat_ids, row_in].set(jnp.arange(assigns, dtype=jnp.int32))
    token_pad = jnp.concatenate([tokens, jnp.zeros((1, D), jnp.bfloat16)], axis=0)
    scaled = (gate_probs[:, :, None] * cotangent.astype(jnp.float32)[:, None, :]).astype(jnp.bfloat16)
    scaled_pad = jnp.concatenate([scaled.reshape(assigns, D), jnp.zeros((1, D), jnp.bfloat16)], axis=0)

    def expert_step(expert_index):
        row_ids = row_table[expert_index]
        token_rows = token_pad[row_ids // TOPK]
        scaled_rows = scaled_pad[row_ids]
        gate_mat = w_gate[expert_index]
        up_mat = w_up[expert_index]
        down_mat = w_down[expert_index]
        gate_pre = jnp.dot(token_rows, gate_mat, preferred_element_type=jnp.float32)
        up_pre = jnp.dot(token_rows, up_mat, preferred_element_type=jnp.float32)
        logistic = jax.nn.sigmoid(gate_pre)
        swish = gate_pre * logistic
        hidden = (swish * up_pre).astype(jnp.bfloat16)
        expert_out = jnp.dot(hidden, down_mat, preferred_element_type=jnp.float32).astype(jnp.bfloat16)
        hidden_grad = jnp.dot(scaled_rows, down_mat.T, preferred_element_type=jnp.float32)
        slope = logistic * (1.0 + gate_pre * (1.0 - logistic))
        gate_grad = (hidden_grad * up_pre * slope).astype(jnp.bfloat16)
        up_grad = (hidden_grad * swish).astype(jnp.bfloat16)
        grad_down = jnp.dot(hidden.T, scaled_rows, preferred_element_type=jnp.float32).astype(jnp.bfloat16)
        grad_gate = jnp.dot(token_rows.T, gate_grad, preferred_element_type=jnp.float32).astype(jnp.bfloat16)
        grad_up = jnp.dot(token_rows.T, up_grad, preferred_element_type=jnp.float32).astype(jnp.bfloat16)
        input_grad = (jnp.dot(gate_grad, gate_mat.T, preferred_element_type=jnp.float32)
                      + jnp.dot(up_grad, up_mat.T, preferred_element_type=jnp.float32)).astype(jnp.bfloat16)
        return expert_out, input_grad, grad_gate, grad_up, grad_down

    outs_all, inputs_all, grad_w_gate, grad_w_up, grad_w_down = lax.map(
        expert_step, jnp.arange(EXPERTS, dtype=jnp.int32))
    where = (flat_ids * capacity + row_in).astype(jnp.int32)
    out_sel = outs_all.reshape(-1, D)[where].reshape(TOKENS, TOPK, D).astype(jnp.float32)
    input_sel = inputs_all.reshape(-1, D)[where].reshape(TOKENS, TOPK, D).astype(jnp.float32)
    layer_out = jnp.sum(gate_probs[:, :, None] * out_sel, axis=1).astype(jnp.bfloat16)
    grad_probs = jnp.sum(cotangent.astype(jnp.float32)[:, None, :] * out_sel, axis=2)
    grad_tokens = jnp.sum(input_sel, axis=1).astype(jnp.bfloat16)
    return layer_out, grad_tokens, grad_probs, grad_w_gate, grad_w_up, grad_w_down
```

```python
import functools
import jax
import jax.numpy as jnp
from jax import lax
from jax.experimental import pallas as pl
from jax.experimental.pallas import tpu as pltpu
from jax.sharding import PartitionSpec as P

BF16 = jnp.bfloat16
F32 = jnp.float32
SLOTS = 12
ROWS = 2 * SLOTS
GROUP = 16
TILE = GROUP * ROWS
VMEM_BYTES = 52 * 1024 * 1024

NN = (((1,), (0,)), ((), ()))
NT = (((1,), (1,)), ((), ()))
TN = (((0,), (0,)), ((), ()))


def dot(a, b, dims=NN):
    return lax.dot_general(a, b, dims, preferred_element_type=F32)


def params():
    return pltpu.CompilerParams(
        vmem_limit_bytes=VMEM_BYTES, dimension_semantics=("arbitrary",)
    )


def cost(flops, nbytes):
    return pl.CostEstimate(flops=int(flops), bytes_accessed=int(nbytes), transcendentals=0)


def spread(rows_of):
    return jnp.concatenate(
        [jnp.broadcast_to(rows_of[i : i + 1], (ROWS, rows_of.shape[1])) for i in range(GROUP)], axis=0
    )


def routing(route_ref, first):
    top, toks = route_ref.shape
    route = route_ref[...]
    ids = lax.broadcasted_iota(jnp.int32, (GROUP, toks), 0) + first
    hits = [jnp.broadcast_to(route[k : k + 1], (GROUP, toks)) == ids for k in range(top)]
    named = sum(h.astype(F32) for h in hits)
    return named, hits


def selection(named):
    toks = named.shape[1]
    before = (
        lax.broadcasted_iota(jnp.int32, (toks, toks), 0)
        < lax.broadcasted_iota(jnp.int32, (toks, toks), 1)
    ).astype(BF16)
    slot = dot(named.astype(BF16), before)
    code = jnp.where(named > 0, slot, -100.0)
    code = jnp.concatenate([code, code + float(SLOTS)], axis=1)
    place = lax.broadcasted_iota(jnp.int32, (ROWS, 2 * toks), 0).astype(F32)
    place = jnp.concatenate([place] * GROUP, axis=0)
    return spread(code) == place


def probs_of(hits, probs_ref):
    probs = probs_ref[...]
    chosen = sum(
        jnp.where(h, jnp.broadcast_to(probs[k : k + 1], h.shape), 0.0) for k, h in enumerate(hits)
    )
    return spread(jnp.concatenate([chosen, chosen], axis=1))


def stacked(x):
    half = x.shape[1] // 2
    return jnp.concatenate([x[:, :half], x[:, half:]], axis=0)


def send_kernel(scaled, route_ref, probs_ref, rows_ref, out_ref):
    named, hits = routing(route_ref, pl.program_id(0) * GROUP)
    sel = selection(named)
    picked = dot(sel.astype(F32).astype(BF16), stacked(rows_ref[...]))
    if scaled:
        weight = jnp.sum(jnp.where(sel, probs_of(hits, probs_ref), 0.0), axis=1, keepdims=True)
        picked = picked * weight
    out_ref[...] = picked.astype(BF16)


def send_rows(scaled, route_t, probs_t, rows, experts):
    toks, width = rows.shape
    top = route_t.shape[0]
    half = width // 2
    return pl.pallas_call(
        functools.partial(send_kernel, scaled),
        grid=(experts // GROUP,),
        in_specs=[
            pl.BlockSpec((top, toks), lambda i: (0, 0)),
            pl.BlockSpec((top, toks), lambda i: (0, 0)),
            pl.BlockSpec((toks, width), lambda i: (0, 0)),
        ],
        out_specs=pl.BlockSpec((TILE, half), lambda i: (i, 0)),
        out_shape=jax.ShapeDtypeStruct((experts * ROWS, half), BF16),
        compiler_params=params(),
        cost_estimate=cost(2 * experts * ROWS * 2 * toks * half, experts * ROWS * half * 2),
        name="send_scaled" if scaled else "send_tokens",
    )(route_t, probs_t, rows)


SUB = 8


def ordering():
    n = SUB * ROWS
    row = lax.broadcasted_iota(jnp.int32, (n, n), 0)
    col = lax.broadcasted_iota(jnp.int32, (n, n), 1)
    upper = (row >= n // 2).astype(jnp.int32)
    within = row - upper * (n // 2)
    source = (within * 43) >> 9
    return (col == SLOTS * source + SLOTS * upper + within).astype(F32).astype(BF16)


def put_in_order(own_ref, other_ref, mine, step, held, out_ref):
    order = ordering()
    n = SUB * ROWS
    for which, ref in ((mine, own_ref), (1 - mine, other_ref)):
        for b in range(GROUP // SUB):
            both = dot(order, ref[b * n : (b + 1) * n, :]).astype(BF16)
            at = pl.multiple_of(step * (GROUP * SLOTS) + b * (n // 2), n // 2)
            for h in range(2):
                part = both[h * (n // 2) : (h + 1) * (n // 2)]
                held[2 * which + h, pl.ds(at, n // 2), :] = part
                out_ref[2 * which + h, b * (n // 2) : (b + 1) * (n // 2), :] = part


def forward_kernel(
    steps, ff_steps, mine_ref, own_ref, other_ref, gate_w, up_w, down_w,
    gate_ref, up_ref, hidden_ref, rows_ref, far_ref, near_ref, held, hidden_all,
):
    i = pl.program_id(0)
    mine = mine_ref[0]
    quarter = own_ref.shape[1]

    @pl.when(i < steps)
    def _():
        put_in_order(own_ref, other_ref, mine, i, held, rows_ref)

    for f in range(ff_steps):
        @pl.when(i == steps + f)
        def _():
            gate = sum(dot(held[q], gate_w[q * quarter : (q + 1) * quarter, :]) for q in range(4))
            up = sum(dot(held[q], up_w[q * quarter : (q + 1) * quarter, :]) for q in range(4))
            gate_ref[...] = gate
            up_ref[...] = up
            hidden = (gate * jax.nn.sigmoid(gate) * up).astype(BF16)
            hidden_ref[...] = hidden
            wide = hidden.shape[1]
            hidden_all[:, f * wide : (f + 1) * wide] = hidden

    @pl.when(jnp.logical_and(i >= steps + ff_steps, i < steps + ff_steps + 2))
    def _():
        far_ref[...] = dot(hidden_all[...], down_w[...]).astype(BF16)

    @pl.when(i >= steps + ff_steps + 2)
    def _():
        near_ref[...] = dot(hidden_all[...], down_w[...])


def quarter_of(i, start, mine):
    q = jnp.clip(i - start, 0, 3)
    return jnp.where(q < 2, 2 * (1 - mine[0]) + q, 2 * mine[0] + q - 2)


def forward(mine, own, other, gate_w, up_w, down_w):
    raw, quarter = own.shape
    model, ff = gate_w.shape
    rows = raw // 2
    steps, ff_steps = raw // TILE, 2
    wide = ff // ff_steps
    last = steps + ff_steps
    ffi = lambda i, m: (0, jnp.clip(i - steps, 0, ff_steps - 1))
    step_rows = GROUP * SLOTS
    return pl.pallas_call(
        functools.partial(forward_kernel, steps, ff_steps),
        grid_spec=pltpu.PrefetchScalarGridSpec(
            num_scalar_prefetch=1,
            grid=(last + 4,),
            in_specs=[
                pl.BlockSpec((TILE, quarter), lambda i, m: (jnp.minimum(i, steps - 1), 0)),
                pl.BlockSpec((TILE, quarter), lambda i, m: (jnp.minimum(i, steps - 1), 0)),
                pl.BlockSpec((model, wide), ffi),
                pl.BlockSpec((model, wide), ffi),
                pl.BlockSpec((ff, quarter), lambda i, m: (0, quarter_of(i, last, m))),
            ],
            out_specs=[
                pl.BlockSpec((rows, wide), ffi),
                pl.BlockSpec((rows, wide), ffi),
                pl.BlockSpec((rows, wide), ffi),
                pl.BlockSpec((4, step_rows, quarter), lambda i, m: (0, jnp.minimum(i, steps - 1), 0)),
                pl.BlockSpec((rows, quarter), lambda i, m: (0, jnp.clip(i - last, 0, 1))),
                pl.BlockSpec((rows, quarter), lambda i, m: (0, jnp.clip(i - last - 2, 0, 1))),
            ],
            scratch_shapes=[pltpu.VMEM((4, rows, quarter), BF16), pltpu.VMEM((rows, ff), BF16)],
        ),
        out_shape=[
            jax.ShapeDtypeStruct((rows, ff), F32),
            jax.ShapeDtypeStruct((rows, ff), F32),
            jax.ShapeDtypeStruct((rows, ff), BF16),
            jax.ShapeDtypeStruct((4, rows, quarter), BF16),
            jax.ShapeDtypeStruct((rows, 2 * quarter), BF16),
            jax.ShapeDtypeStruct((rows, 2 * quarter), F32),
        ],
        compiler_params=params(),
        cost_estimate=cost(6 * rows * model * ff, 6 * model * ff + 30e6),
        name="expert_forward",
    )(mine, own, other, gate_w, up_w, down_w)


def backward_kernel(
    steps, ff_steps, mine_ref, own_ref, other_ref, down_w, gate_ref, up_ref, gate_w, up_w,
    gate_grad_ref, up_grad_ref, rows_ref, far_ref, near_ref, held, gate_grads, up_grads,
):
    i = pl.program_id(0)
    mine = mine_ref[0]
    quarter = own_ref.shape[1]

    @pl.when(i < steps)
    def _():
        put_in_order(own_ref, other_ref, mine, i, held, rows_ref)

    for f in range(ff_steps):
        @pl.when(i == steps + f)
        def _():
            hidden_grad = sum(
                dot(held[q], down_w[:, q * quarter : (q + 1) * quarter], NT) for q in range(4)
            )
            gate, up = gate_ref[...], up_ref[...]
            logistic = jax.nn.sigmoid(gate)
            gate_grad = (hidden_grad * up * logistic * (1.0 + gate * (1.0 - logistic))).astype(BF16)
            up_grad = (hidden_grad * (gate * logistic)).astype(BF16)
            gate_grad_ref[...] = gate_grad
            up_grad_ref[...] = up_grad
            wide = gate_grad.shape[1]
            gate_grads[:, f * wide : (f + 1) * wide] = gate_grad
            up_grads[:, f * wide : (f + 1) * wide] = up_grad

    @pl.when(jnp.logical_and(i >= steps + ff_steps, i < steps + ff_steps + 2))
    def _():
        far_ref[...] = (
            dot(gate_grads[...], gate_w[...], NT) + dot(up_grads[...], up_w[...], NT)
        ).astype(BF16)

    @pl.when(i >= steps + ff_steps + 2)
    def _():
        near_ref[...] = dot(gate_grads[...], gate_w[...], NT) + dot(up_grads[...], up_w[...], NT)


def backward(mine, own, other, down_w, gate_pre, up_pre, gate_w, up_w):
    raw, quarter = own.shape
    model, ff = gate_w.shape
    rows = raw // 2
    steps, ff_steps = raw // TILE, 2
    wide = ff // ff_steps
    last = steps + ff_steps
    ffi = lambda i, m: (0, jnp.clip(i - steps, 0, ff_steps - 1))
    step_rows = GROUP * SLOTS
    return pl.pallas_call(
        functools.partial(backward_kernel, steps, ff_steps),
        grid_spec=pltpu.PrefetchScalarGridSpec(
            num_scalar_prefetch=1,
            grid=(last + 4,),
            in_specs=[
                pl.BlockSpec((TILE, quarter), lambda i, m: (jnp.minimum(i, steps - 1), 0)),
                pl.BlockSpec((TILE, quarter), lambda i, m: (jnp.minimum(i, steps - 1), 0)),
                pl.BlockSpec((wide, model), lambda i, m: (jnp.clip(i - steps, 0, ff_steps - 1), 0)),
                pl.BlockSpec((rows, wide), ffi),
                pl.BlockSpec((rows, wide), ffi),
                pl.BlockSpec((quarter, ff), lambda i, m: (quarter_of(i, last, m), 0)),
                pl.BlockSpec((quarter, ff), lambda i, m: (quarter_of(i, last, m), 0)),
            ],
            out_specs=[
                pl.BlockSpec((rows, wide), ffi),
                pl.BlockSpec((rows, wide), ffi),
                pl.BlockSpec((4, step_rows, quarter), lambda i, m: (0, jnp.minimum(i, steps - 1), 0)),
                pl.BlockSpec((rows, quarter), lambda i, m: (0, jnp.clip(i - last, 0, 1))),
                pl.BlockSpec((rows, quarter), lambda i, m: (0, jnp.clip(i - last - 2, 0, 1))),
            ],
            scratch_shapes=[
                pltpu.VMEM((4, rows, quarter), BF16),
                pltpu.VMEM((rows, ff), BF16),
                pltpu.VMEM((rows, ff), BF16),
            ],
        ),
        out_shape=[
            jax.ShapeDtypeStruct((rows, ff), BF16),
            jax.ShapeDtypeStruct((rows, ff), BF16),
            jax.ShapeDtypeStruct((4, rows, quarter), BF16),
            jax.ShapeDtypeStruct((rows, 2 * quarter), BF16),
            jax.ShapeDtypeStruct((rows, 2 * quarter), F32),
        ],
        compiler_params=params(),
        cost_estimate=cost(6 * rows * model * ff, 6 * model * ff + 30e6),
        name="expert_backward",
    )(mine, own, other, down_w, gate_pre, up_pre, gate_w, up_w)


def pack_kernel(near_ref, far_ref, out_ref):
    order = ordering()
    n = SUB * ROWS
    quarter = out_ref.shape[1]
    for b in range(GROUP // SUB):
        at = slice(b * (n // 2), (b + 1) * (n // 2))
        total = (near_ref[at, :] + far_ref[at, :].astype(F32)).astype(BF16)
        both = jnp.concatenate([total[:, :quarter], total[:, quarter:]], axis=0)
        out_ref[b * n : (b + 1) * n, :] = dot(order, both, TN).astype(BF16)


def pack(near, far):
    rows, width = near.shape
    step_rows = GROUP * SLOTS
    return pl.pallas_call(
        pack_kernel,
        grid=(rows // step_rows,),
        in_specs=[pl.BlockSpec((step_rows, width), lambda i: (i, 0))] * 2,
        out_specs=pl.BlockSpec((TILE, width // 2), lambda i: (i, 0)),
        out_shape=jax.ShapeDtypeStruct((2 * rows, width // 2), BF16),
        compiler_params=params(),
        cost_estimate=cost(2 * rows * width * SUB * ROWS, 8 * rows * width),
        name="pack",
    )(near, far)


def weights_kernel(rows_ref, scaled_ref, hidden_ref, gate_grad_ref, up_grad_ref, gate_w, up_w, down_w):
    rows = rows_ref[0]
    gate_w[...] = dot(rows, gate_grad_ref[...], TN).astype(BF16)
    up_w[...] = dot(rows, up_grad_ref[...], TN).astype(BF16)
    down_w[...] = dot(hidden_ref[...], scaled_ref[0], TN).astype(BF16)


def weight_grads(token_rows, scaled_rows, hidden, gate_grad, up_grad):
    quarters, rows, quarter = token_rows.shape
    ff = hidden.shape[1]
    whole = pl.BlockSpec((rows, ff), lambda i: (0, 0))
    part = pl.BlockSpec((1, rows, quarter), lambda i: (i, 0, 0))
    return pl.pallas_call(
        weights_kernel,
        grid=(quarters,),
        in_specs=[part, part, whole, whole, whole],
        out_specs=[
            pl.BlockSpec((quarter, ff), lambda i: (i, 0)),
            pl.BlockSpec((quarter, ff), lambda i: (i, 0)),
            pl.BlockSpec((ff, quarter), lambda i: (0, i)),
        ],
        out_shape=[
            jax.ShapeDtypeStruct((quarters * quarter, ff), BF16),
            jax.ShapeDtypeStruct((quarters * quarter, ff), BF16),
            jax.ShapeDtypeStruct((ff, quarters * quarter), BF16),
        ],
        compiler_params=params(),
        cost_estimate=cost(6 * rows * quarters * quarter * ff, 10 * quarters * quarter * ff),
        name="weight_grads",
    )(token_rows, scaled_rows, hidden, gate_grad, up_grad)


def outputs_kernel(route_ref, probs_ref, cot_ref, back_ref, out_ref, grad_ref, total):
    i = pl.program_id(0)

    @pl.when(i == 0)
    def _():
        total[...] = jnp.zeros_like(total)
        grad_ref[...] = jnp.zeros_like(grad_ref)

    toks = cot_ref.shape[0]
    half = back_ref.shape[1]
    named, hits = routing(route_ref, i * GROUP)
    sel = selection(named)
    weight = jnp.where(sel, probs_of(hits, probs_ref), 0.0)
    high = weight.astype(BF16)
    low = (weight - high.astype(F32)).astype(BF16)
    back = back_ref[...]
    total[...] += dot(high, back, TN) + dot(low, back, TN)
    products = jnp.where(sel, dot(back, stacked(cot_ref[...]), NT), 0.0)
    sums = jnp.concatenate(
        [
            jnp.sum(products[e * ROWS : (e + 1) * ROWS], axis=0, keepdims=True)
            for e in range(GROUP)
        ],
        axis=0,
    )
    sums = sums[:, :toks] + sums[:, toks:]
    grad_ref[...] += jnp.concatenate(
        [jnp.sum(jnp.where(h, sums, 0.0), axis=0, keepdims=True) for h in hits], axis=0
    )

    @pl.when(i == pl.num_programs(0) - 1)
    def _():
        out_ref[:, :half] = total[:toks].astype(BF16)
        out_ref[:, half:] = total[toks:].astype(BF16)


def token_outputs(route_t, probs_t, cot, back):
    toks, width = cot.shape
    top = route_t.shape[0]
    steps = back.shape[0] // TILE
    small = pl.BlockSpec((top, toks), lambda i: (0, 0))
    wide = pl.BlockSpec((toks, width), lambda i: (0, 0))
    return pl.pallas_call(
        outputs_kernel,
        grid=(steps,),
        in_specs=[small, small, wide, pl.BlockSpec((TILE, width // 2), lambda i: (i, 0))],
        out_specs=[wide, small],
        out_shape=[
            jax.ShapeDtypeStruct((toks, width), BF16),
            jax.ShapeDtypeStruct((top, toks), F32),
        ],
        scratch_shapes=[pltpu.VMEM((2 * toks, width // 2), F32)],
        compiler_params=params(),
        cost_estimate=cost(6 * back.shape[0] * 2 * toks * width // 2, 3 * back.shape[0] * width),
        name="token_outputs",
    )(route_t, probs_t, cot, back)


def inputs_kernel(route_ref, back_ref, out_ref, total):
    i = pl.program_id(0)

    @pl.when(i == 0)
    def _():
        total[...] = jnp.zeros_like(total)

    toks = out_ref.shape[0]
    half = back_ref.shape[1]
    named, _ = routing(route_ref, i * GROUP)
    sel = selection(named).astype(F32).astype(BF16)
    total[...] += dot(sel, back_ref[...], TN)

    @pl.when(i == pl.num_programs(0) - 1)
    def _():
        out_ref[:, :half] = total[:toks].astype(BF16)
        out_ref[:, half:] = total[toks:].astype(BF16)


def token_grads(route_t, back):
    top, toks = route_t.shape
    width = 2 * back.shape[1]
    steps = back.shape[0] // TILE
    return pl.pallas_call(
        inputs_kernel,
        grid=(steps,),
        in_specs=[
            pl.BlockSpec((top, toks), lambda i: (0, 0)),
            pl.BlockSpec((TILE, width // 2), lambda i: (i, 0)),
        ],
        out_specs=pl.BlockSpec((toks, width), lambda i: (0, 0)),
        out_shape=jax.ShapeDtypeStruct((toks, width), BF16),
        scratch_shapes=[pltpu.VMEM((2 * toks, width // 2), F32)],
        compiler_params=params(),
        cost_estimate=cost(2 * back.shape[0] * 2 * toks * width // 2, back.shape[0] * width),
        name="token_grads",
    )(route_t, back)


def exchange(x):
    experts = lax.axis_size("expert")
    y = lax.all_to_all(
        x.reshape(experts, ROWS, -1), "expert", split_axis=0, concat_axis=0, tiled=True
    )
    return y.reshape(x.shape)


def swap(x):
    return lax.ppermute(x, "mp", [(0, 1), (1, 0)])


def body(tokens, cotangent, route_ids, gate_probs, w_gate, w_up, w_down):
    experts = lax.axis_size("expert")
    mine = lax.axis_index("mp").astype(jnp.int32).reshape(1)
    route_t, probs_t = route_ids.T, gate_probs.T
    gate_w, up_w, down_w = w_gate[0], w_up[0], w_down[0]

    got_tokens = exchange(send_rows(False, route_t, probs_t, tokens, experts))
    got_scaled = exchange(send_rows(True, route_t, probs_t, cotangent, experts))

    gate_pre, up_pre, hidden, token_rows, out_far, out_near = forward(
        mine, got_tokens, swap(got_tokens), gate_w, up_w, down_w
    )
    back_out = exchange(pack(out_near, swap(out_far)))

    gate_grad, up_grad, scaled_rows, in_far, in_near = backward(
        mine, got_scaled, swap(got_scaled), down_w, gate_pre, up_pre, gate_w, up_w
    )
    back_in = exchange(pack(in_near, swap(in_far)))

    grad_w_gate, grad_w_up, grad_w_down = weight_grads(
        token_rows, scaled_rows, hidden, gate_grad, up_grad
    )
    layer_out, grad_part = token_outputs(route_t, probs_t, cotangent, back_out)
    grad_probs = lax.psum(grad_part, "mp").T
    grad_tokens = token_grads(route_t, back_in)
    return (
        layer_out, grad_tokens, grad_probs, grad_w_gate[None], grad_w_up[None], grad_w_down[None],
    )


def solution(mesh):
    return jax.shard_map(
        body,
        mesh=mesh,
        in_specs=(
            P("expert", "mp"),
            P("expert", "mp"),
            P("expert", None),
            P("expert", None),
            P("expert", None, "mp"),
            P("expert", None, "mp"),
            P("expert", "mp", None),
        ),
        out_specs=(
            P("expert", "mp"),
            P("expert", "mp"),
            P("expert", None),
            P("expert", None, "mp"),
            P("expert", None, "mp"),
            P("expert", "mp", None),
        ),
        check_vma=False,
    )
```

```python
import functools
import jax
import jax.numpy as jnp
from jax import lax
from jax.experimental import pallas as pl
from jax.experimental.pallas import tpu as pltpu
from jax.sharding import PartitionSpec as P

BF16 = jnp.bfloat16
F32 = jnp.float32
SLOTS = 12
ROWS = 2 * SLOTS
GROUP = 16
TILE = GROUP * ROWS
VMEM_BYTES = 52 * 1024 * 1024

NN = (((1,), (0,)), ((), ()))
NT = (((1,), (1,)), ((), ()))
TN = (((0,), (0,)), ((), ()))


def dot(a, b, dims=NN):
    return lax.dot_general(a, b, dims, preferred_element_type=F32)


def params():
    return pltpu.CompilerParams(
        vmem_limit_bytes=VMEM_BYTES, dimension_semantics=("arbitrary",)
    )


def cost():
    return pl.CostEstimate(flops=1, bytes_accessed=1, transcendentals=0)


def spread(rows_of):
    return jnp.concatenate(
        [jnp.broadcast_to(rows_of[i : i + 1], (ROWS, rows_of.shape[1])) for i in range(GROUP)], axis=0
    )


def routing(route_ref, first):
    top, toks = route_ref.shape
    route = route_ref[...]
    ids = lax.broadcasted_iota(jnp.int32, (GROUP, toks), 0) + first
    hits = [jnp.broadcast_to(route[k : k + 1], (GROUP, toks)) == ids for k in range(top)]
    named = sum(h.astype(F32) for h in hits)
    return named, hits


def selection(named):
    toks = named.shape[1]
    before = (
        lax.broadcasted_iota(jnp.int32, (toks, toks), 0)
        < lax.broadcasted_iota(jnp.int32, (toks, toks), 1)
    ).astype(BF16)
    slot = dot(named.astype(BF16), before)
    code = jnp.where(named > 0, slot, -100.0)
    code = jnp.concatenate([code, code + float(SLOTS)], axis=1)
    place = lax.broadcasted_iota(jnp.int32, (ROWS, 2 * toks), 0).astype(F32)
    place = jnp.concatenate([place] * GROUP, axis=0)
    return spread(code) == place


def probs_of(hits, probs_ref):
    probs = probs_ref[...]
    chosen = sum(
        jnp.where(h, jnp.broadcast_to(probs[k : k + 1], h.shape), 0.0) for k, h in enumerate(hits)
    )
    return spread(jnp.concatenate([chosen, chosen], axis=1))


def stacked(x):
    half = x.shape[1] // 2
    return jnp.concatenate([x[:, :half], x[:, half:]], axis=0)


def send_kernel(scaled, route_ref, probs_ref, rows_ref, out_ref):
    named, hits = routing(route_ref, pl.program_id(0) * GROUP)
    sel = selection(named)
    picked = dot(sel.astype(F32).astype(BF16), stacked(rows_ref[...]))
    if scaled:
        weight = jnp.sum(jnp.where(sel, probs_of(hits, probs_ref), 0.0), axis=1, keepdims=True)
        picked = picked * weight
    out_ref[...] = picked.astype(BF16)


def send_rows(scaled, route_t, probs_t, rows, experts):
    toks, width = rows.shape
    top = route_t.shape[0]
    half = width // 2
    return pl.pallas_call(
        functools.partial(send_kernel, scaled),
        grid=(experts // GROUP,),
        in_specs=[
            pl.BlockSpec((top, toks), lambda i: (0, 0)),
            pl.BlockSpec((top, toks), lambda i: (0, 0)),
            pl.BlockSpec((toks, width), lambda i: (0, 0)),
        ],
        out_specs=pl.BlockSpec((TILE, half), lambda i: (i, 0)),
        out_shape=jax.ShapeDtypeStruct((experts * ROWS, half), BF16),
        compiler_params=params(),
        cost_estimate=cost(),
        name="send_scaled" if scaled else "send_tokens",
    )(route_t, probs_t, rows)


SUB = 8


def ordering():
    n = SUB * ROWS
    row = lax.broadcasted_iota(jnp.int32, (n, n), 0)
    col = lax.broadcasted_iota(jnp.int32, (n, n), 1)
    upper = (row >= n // 2).astype(jnp.int32)
    within = row - upper * (n // 2)
    source = (within * 43) >> 9
    return (col == SLOTS * source + SLOTS * upper + within).astype(F32).astype(BF16)


def put_in_order(own_ref, other_ref, mine, step, held, out_ref):
    order = ordering()
    n = SUB * ROWS
    for which, ref in ((mine, own_ref), (1 - mine, other_ref)):
        for b in range(GROUP // SUB):
            both = dot(order, ref[b * n : (b + 1) * n, :]).astype(BF16)
            at = pl.multiple_of(step * (GROUP * SLOTS) + b * (n // 2), n // 2)
            for h in range(2):
                part = both[h * (n // 2) : (h + 1) * (n // 2)]
                held[2 * which + h, pl.ds(at, n // 2), :] = part
                out_ref[2 * which + h, b * (n // 2) : (b + 1) * (n // 2), :] = part


def put_all_in_order(i, steps, own_ref, others, mine, held, out_ref):
    each = steps // len(others)
    for p, ref in enumerate(others):
        @pl.when(jnp.logical_and(i >= p * each, i < (p + 1) * each))
        def _():
            put_in_order(own_ref, ref, mine, i, held, out_ref)


def piece_specs(quarter, steps, pieces):
    each = steps // pieces
    return [
        pl.BlockSpec((TILE, quarter), lambda i, m, p=p: (jnp.clip(i - p * each, 0, each - 1), 0))
        for p in range(pieces)
    ]


def forward_kernel(
    steps, ff_steps, mine_ref, own_ref, other0, other1, gate_w, up_w, down_w,
    gate_ref, up_ref, hidden_ref, rows_ref, far0, far1, near_ref, held, hidden_all,
):
    i = pl.program_id(0)
    mine = mine_ref[0]
    quarter = own_ref.shape[1]

    put_all_in_order(i, steps, own_ref, (other0, other1), mine, held, rows_ref)

    for f in range(ff_steps):
        @pl.when(i == steps + f)
        def _():
            gate = sum(dot(held[q], gate_w[q * quarter : (q + 1) * quarter, :]) for q in range(4))
            up = sum(dot(held[q], up_w[q * quarter : (q + 1) * quarter, :]) for q in range(4))
            gate_ref[...] = gate
            up_ref[...] = up
            hidden = (gate * jax.nn.sigmoid(gate) * up).astype(BF16)
            hidden_ref[...] = hidden
            wide = hidden.shape[1]
            hidden_all[:, f * wide : (f + 1) * wide] = hidden

    for h, far_ref in enumerate((far0, far1)):
        @pl.when(i == steps + ff_steps + h)
        def _():
            far_ref[...] = dot(hidden_all[...], down_w[...]).astype(BF16)

    @pl.when(i >= steps + ff_steps + 2)
    def _():
        near_ref[...] = dot(hidden_all[...], down_w[...])


def quarter_of(i, start, mine):
    q = jnp.clip(i - start, 0, 3)
    return jnp.where(q < 2, 2 * (1 - mine[0]) + q, 2 * mine[0] + q - 2)


def forward(mine, own, others, gate_w, up_w, down_w):
    raw, quarter = own.shape
    model, ff = gate_w.shape
    rows = raw // 2
    steps, ff_steps = raw // TILE, 2
    wide = ff // ff_steps
    last = steps + ff_steps
    ffi = lambda i, m: (0, jnp.clip(i - steps, 0, ff_steps - 1))
    step_rows = GROUP * SLOTS
    return pl.pallas_call(
        functools.partial(forward_kernel, steps, ff_steps),
        grid_spec=pltpu.PrefetchScalarGridSpec(
            num_scalar_prefetch=1,
            grid=(last + 4,),
            in_specs=[
                pl.BlockSpec((TILE, quarter), lambda i, m: (jnp.minimum(i, steps - 1), 0)),
                *piece_specs(quarter, steps, len(others)),
                pl.BlockSpec((model, wide), ffi),
                pl.BlockSpec((model, wide), ffi),
                pl.BlockSpec((ff, quarter), lambda i, m: (0, quarter_of(i, last, m))),
            ],
            out_specs=[
                pl.BlockSpec((rows, wide), ffi),
                pl.BlockSpec((rows, wide), ffi),
                pl.BlockSpec((rows, wide), ffi),
                pl.BlockSpec((4, step_rows, quarter), lambda i, m: (0, jnp.minimum(i, steps - 1), 0)),
                pl.BlockSpec((rows, quarter), lambda i, m: (0, 0)),
                pl.BlockSpec((rows, quarter), lambda i, m: (0, 0)),
                pl.BlockSpec((rows, quarter), lambda i, m: (0, jnp.clip(i - last - 2, 0, 1))),
            ],
            scratch_shapes=[pltpu.VMEM((4, rows, quarter), BF16), pltpu.VMEM((rows, ff), BF16)],
        ),
        out_shape=[
            jax.ShapeDtypeStruct((rows, ff), F32),
            jax.ShapeDtypeStruct((rows, ff), F32),
            jax.ShapeDtypeStruct((rows, ff), BF16),
            jax.ShapeDtypeStruct((4, rows, quarter), BF16),
            jax.ShapeDtypeStruct((rows, quarter), BF16),
            jax.ShapeDtypeStruct((rows, quarter), BF16),
            jax.ShapeDtypeStruct((rows, 2 * quarter), F32),
        ],
        compiler_params=params(),
        cost_estimate=cost(),
        name="expert_forward",
    )(mine, own, *others, gate_w, up_w, down_w)


def backward_kernel(
    steps, ff_steps, mine_ref, own_ref, other0, other1, down_w, gate_ref, up_ref, gate_w, up_w,
    gate_grad_ref, up_grad_ref, rows_ref, far0, far1, near_ref, held, gate_grads, up_grads,
):
    i = pl.program_id(0)
    mine = mine_ref[0]
    quarter = own_ref.shape[1]

    put_all_in_order(i, steps, own_ref, (other0, other1), mine, held, rows_ref)

    for f in range(ff_steps):
        @pl.when(i == steps + f)
        def _():
            hidden_grad = sum(
                dot(held[q], down_w[:, q * quarter : (q + 1) * quarter], NT) for q in range(4)
            )
            gate, up = gate_ref[...], up_ref[...]
            logistic = jax.nn.sigmoid(gate)
            gate_grad = (hidden_grad * up * logistic * (1.0 + gate * (1.0 - logistic))).astype(BF16)
            up_grad = (hidden_grad * (gate * logistic)).astype(BF16)
            gate_grad_ref[...] = gate_grad
            up_grad_ref[...] = up_grad
            wide = gate_grad.shape[1]
            gate_grads[:, f * wide : (f + 1) * wide] = gate_grad
            up_grads[:, f * wide : (f + 1) * wide] = up_grad

    for h, far_ref in enumerate((far0, far1)):
        @pl.when(i == steps + ff_steps + h)
        def _():
            far_ref[...] = (
                dot(gate_grads[...], gate_w[...], NT) + dot(up_grads[...], up_w[...], NT)
            ).astype(BF16)

    @pl.when(i >= steps + ff_steps + 2)
    def _():
        near_ref[...] = dot(gate_grads[...], gate_w[...], NT) + dot(up_grads[...], up_w[...], NT)


def backward(mine, own, others, down_w, gate_pre, up_pre, gate_w, up_w):
    raw, quarter = own.shape
    model, ff = gate_w.shape
    rows = raw // 2
    steps, ff_steps = raw // TILE, 2
    wide = ff // ff_steps
    last = steps + ff_steps
    ffi = lambda i, m: (0, jnp.clip(i - steps, 0, ff_steps - 1))
    step_rows = GROUP * SLOTS
    return pl.pallas_call(
        functools.partial(backward_kernel, steps, ff_steps),
        grid_spec=pltpu.PrefetchScalarGridSpec(
            num_scalar_prefetch=1,
            grid=(last + 4,),
            in_specs=[
                pl.BlockSpec((TILE, quarter), lambda i, m: (jnp.minimum(i, steps - 1), 0)),
                *piece_specs(quarter, steps, len(others)),
                pl.BlockSpec((wide, model), lambda i, m: (jnp.clip(i - steps, 0, ff_steps - 1), 0)),
                pl.BlockSpec((rows, wide), ffi),
                pl.BlockSpec((rows, wide), ffi),
                pl.BlockSpec((quarter, ff), lambda i, m: (quarter_of(i, last, m), 0)),
                pl.BlockSpec((quarter, ff), lambda i, m: (quarter_of(i, last, m), 0)),
            ],
            out_specs=[
                pl.BlockSpec((rows, wide), ffi),
                pl.BlockSpec((rows, wide), ffi),
                pl.BlockSpec((4, step_rows, quarter), lambda i, m: (0, jnp.minimum(i, steps - 1), 0)),
                pl.BlockSpec((rows, quarter), lambda i, m: (0, 0)),
                pl.BlockSpec((rows, quarter), lambda i, m: (0, 0)),
                pl.BlockSpec((rows, quarter), lambda i, m: (0, jnp.clip(i - last - 2, 0, 1))),
            ],
            scratch_shapes=[
                pltpu.VMEM((4, rows, quarter), BF16),
                pltpu.VMEM((rows, ff), BF16),
                pltpu.VMEM((rows, ff), BF16),
            ],
        ),
        out_shape=[
            jax.ShapeDtypeStruct((rows, ff), BF16),
            jax.ShapeDtypeStruct((rows, ff), BF16),
            jax.ShapeDtypeStruct((4, rows, quarter), BF16),
            jax.ShapeDtypeStruct((rows, quarter), BF16),
            jax.ShapeDtypeStruct((rows, quarter), BF16),
            jax.ShapeDtypeStruct((rows, 2 * quarter), F32),
        ],
        compiler_params=params(),
        cost_estimate=cost(),
        name="expert_backward",
    )(mine, own, *others, down_w, gate_pre, up_pre, gate_w, up_w)


def pack_kernel(near_ref, far0, far1, out_ref):
    order = ordering()
    n = SUB * ROWS
    quarter = out_ref.shape[1]
    for b in range(GROUP // SUB):
        at = slice(b * (n // 2), (b + 1) * (n // 2))
        both = jnp.concatenate(
            [
                (near_ref[at, h * quarter : (h + 1) * quarter] + far[at, :].astype(F32)).astype(BF16)
                for h, far in enumerate((far0, far1))
            ],
            axis=0,
        )
        out_ref[b * n : (b + 1) * n, :] = dot(order, both, TN).astype(BF16)


def pack(near, fars):
    rows, width = near.shape
    step_rows = GROUP * SLOTS
    return pl.pallas_call(
        pack_kernel,
        grid=(rows // step_rows,),
        in_specs=[
            pl.BlockSpec((step_rows, width), lambda i: (i, 0)),
            pl.BlockSpec((step_rows, width // 2), lambda i: (i, 0)),
            pl.BlockSpec((step_rows, width // 2), lambda i: (i, 0)),
        ],
        out_specs=pl.BlockSpec((TILE, width // 2), lambda i: (i, 0)),
        out_shape=jax.ShapeDtypeStruct((2 * rows, width // 2), BF16),
        compiler_params=params(),
        cost_estimate=cost(),
        name="pack",
    )(near, *fars)


def weights_kernel(rows_ref, scaled_ref, hidden_ref, gate_grad_ref, up_grad_ref, gate_w, up_w, down_w):
    rows = rows_ref[0]
    gate_w[...] = dot(rows, gate_grad_ref[...], TN).astype(BF16)
    up_w[...] = dot(rows, up_grad_ref[...], TN).astype(BF16)
    down_w[...] = dot(hidden_ref[...], scaled_ref[0], TN).astype(BF16)


def weight_grads(token_rows, scaled_rows, hidden, gate_grad, up_grad):
    quarters, rows, quarter = token_rows.shape
    ff = hidden.shape[1]
    whole = pl.BlockSpec((rows, ff), lambda i: (0, 0))
    part = pl.BlockSpec((1, rows, quarter), lambda i: (i, 0, 0))
    return pl.pallas_call(
        weights_kernel,
        grid=(quarters,),
        in_specs=[part, part, whole, whole, whole],
        out_specs=[
            pl.BlockSpec((quarter, ff), lambda i: (i, 0)),
            pl.BlockSpec((quarter, ff), lambda i: (i, 0)),
            pl.BlockSpec((ff, quarter), lambda i: (0, i)),
        ],
        out_shape=[
            jax.ShapeDtypeStruct((quarters * quarter, ff), BF16),
            jax.ShapeDtypeStruct((quarters * quarter, ff), BF16),
            jax.ShapeDtypeStruct((ff, quarters * quarter), BF16),
        ],
        compiler_params=params(),
        cost_estimate=cost(),
        name="weight_grads",
    )(token_rows, scaled_rows, hidden, gate_grad, up_grad)


def outputs_kernel(route_ref, probs_ref, cot_ref, back_ref, out_ref, grad_ref, total):
    i = pl.program_id(0)

    @pl.when(i == 0)
    def _():
        total[...] = jnp.zeros_like(total)
        grad_ref[...] = jnp.zeros_like(grad_ref)

    toks = cot_ref.shape[0]
    half = back_ref.shape[1]
    named, hits = routing(route_ref, i * GROUP)
    sel = selection(named)
    weight = jnp.where(sel, probs_of(hits, probs_ref), 0.0)
    high = weight.astype(BF16)
    low = (weight - high.astype(F32)).astype(BF16)
    back = back_ref[...]
    total[...] += dot(high, back, TN) + dot(low, back, TN)
    products = jnp.where(sel, dot(back, stacked(cot_ref[...]), NT), 0.0)
    sums = jnp.concatenate(
        [
            jnp.sum(products[e * ROWS : (e + 1) * ROWS], axis=0, keepdims=True)
            for e in range(GROUP)
        ],
        axis=0,
    )
    sums = sums[:, :toks] + sums[:, toks:]
    grad_ref[...] += jnp.concatenate(
        [jnp.sum(jnp.where(h, sums, 0.0), axis=0, keepdims=True) for h in hits], axis=0
    )

    @pl.when(i == pl.num_programs(0) - 1)
    def _():
        out_ref[:, :half] = total[:toks].astype(BF16)
        out_ref[:, half:] = total[toks:].astype(BF16)


def token_outputs(route_t, probs_t, cot, back):
    toks, width = cot.shape
    top = route_t.shape[0]
    steps = back.shape[0] // TILE
    small = pl.BlockSpec((top, toks), lambda i: (0, 0))
    wide = pl.BlockSpec((toks, width), lambda i: (0, 0))
    return pl.pallas_call(
        outputs_kernel,
        grid=(steps,),
        in_specs=[small, small, wide, pl.BlockSpec((TILE, width // 2), lambda i: (i, 0))],
        out_specs=[wide, small],
        out_shape=[
            jax.ShapeDtypeStruct((toks, width), BF16),
            jax.ShapeDtypeStruct((top, toks), F32),
        ],
        scratch_shapes=[pltpu.VMEM((2 * toks, width // 2), F32)],
        compiler_params=params(),
        cost_estimate=cost(),
        name="token_outputs",
    )(route_t, probs_t, cot, back)


def inputs_kernel(route_ref, back_ref, out_ref, total):
    i = pl.program_id(0)

    @pl.when(i == 0)
    def _():
        total[...] = jnp.zeros_like(total)

    toks = out_ref.shape[0]
    half = back_ref.shape[1]
    named, _ = routing(route_ref, i * GROUP)
    sel = selection(named).astype(F32).astype(BF16)
    total[...] += dot(sel, back_ref[...], TN)

    @pl.when(i == pl.num_programs(0) - 1)
    def _():
        out_ref[:, :half] = total[:toks].astype(BF16)
        out_ref[:, half:] = total[toks:].astype(BF16)


def token_grads(route_t, back):
    top, toks = route_t.shape
    width = 2 * back.shape[1]
    steps = back.shape[0] // TILE
    return pl.pallas_call(
        inputs_kernel,
        grid=(steps,),
        in_specs=[
            pl.BlockSpec((top, toks), lambda i: (0, 0)),
            pl.BlockSpec((TILE, width // 2), lambda i: (i, 0)),
        ],
        out_specs=pl.BlockSpec((toks, width), lambda i: (0, 0)),
        out_shape=jax.ShapeDtypeStruct((toks, width), BF16),
        scratch_shapes=[pltpu.VMEM((2 * toks, width // 2), F32)],
        compiler_params=params(),
        cost_estimate=cost(),
        name="token_grads",
    )(route_t, back)


def exchange(x):
    experts = lax.axis_size("expert")
    y = lax.all_to_all(
        x.reshape(experts, ROWS, -1), "expert", split_axis=0, concat_axis=0, tiled=True
    )
    return y.reshape(x.shape)


def swap(*parts):
    return [lax.ppermute(x, "mp", [(0, 1), (1, 0)]) for x in parts]


def halves(x):
    half = x.shape[0] // 2
    return x[:half], x[half:]


def body(tokens, cotangent, route_ids, gate_probs, w_gate, w_up, w_down):
    experts = lax.axis_size("expert")
    mine = lax.axis_index("mp").astype(jnp.int32).reshape(1)
    route_t, probs_t = route_ids.T, gate_probs.T
    gate_w, up_w, down_w = w_gate[0], w_up[0], w_down[0]

    send_tokens = send_rows(False, route_t, probs_t, tokens, experts)
    send_scaled = send_rows(True, route_t, probs_t, cotangent, experts)
    got_tokens, send_scaled = lax.optimization_barrier((exchange(send_tokens), send_scaled))
    got_scaled = exchange(send_scaled)

    gate_pre, up_pre, hidden, token_rows, far0, far1, out_near = forward(
        mine, got_tokens, swap(*halves(got_tokens)), gate_w, up_w, down_w
    )
    send_out = pack(out_near, swap(far0, far1))
    got_scaled, send_out = lax.optimization_barrier((got_scaled, send_out))
    back_out = exchange(send_out)

    gate_grad, up_grad, scaled_rows, far0, far1, in_near = backward(
        mine, got_scaled, swap(*halves(got_scaled)), down_w, gate_pre, up_pre, gate_w, up_w
    )
    send_in = pack(in_near, swap(far0, far1))
    back_out, send_in = lax.optimization_barrier((back_out, send_in))
    back_in = exchange(send_in)

    grad_w_gate, grad_w_up, grad_w_down = weight_grads(
        token_rows, scaled_rows, hidden, gate_grad, up_grad
    )
    layer_out, grad_part = token_outputs(route_t, probs_t, cotangent, back_out)
    grad_probs = lax.psum(grad_part, "mp").T
    grad_tokens = token_grads(route_t, back_in)
    return (
        layer_out, grad_tokens, grad_probs, grad_w_gate[None], grad_w_up[None], grad_w_down[None],
    )


def solution(mesh):
    return jax.shard_map(
        body,
        mesh=mesh,
        in_specs=(
            P("expert", "mp"),
            P("expert", "mp"),
            P("expert", None),
            P("expert", None),
            P("expert", None, "mp"),
            P("expert", None, "mp"),
            P("expert", "mp", None),
        ),
        out_specs=(
            P("expert", "mp"),
            P("expert", "mp"),
            P("expert", None),
            P("expert", None, "mp"),
            P("expert", None, "mp"),
            P("expert", "mp", None),
        ),
        check_vma=False,
    )
```

```python
import functools
import jax
import jax.numpy as jnp
from jax import lax
from jax.experimental import pallas as pl
from jax.experimental.pallas import tpu as pltpu
from jax.sharding import PartitionSpec as P

BF16 = jnp.bfloat16
F32 = jnp.float32
SLOTS = 12
ROWS = 2 * SLOTS
GROUP = 16
TILE = GROUP * ROWS

NN = (((1,), (0,)), ((), ()))
NT = (((1,), (1,)), ((), ()))
TN = (((0,), (0,)), ((), ()))


def dot(a, b, dims=NN):
    return lax.dot_general(a, b, dims, preferred_element_type=F32)


def params(mebibytes):
    return pltpu.CompilerParams(
        vmem_limit_bytes=mebibytes * 1024 * 1024, dimension_semantics=("arbitrary",)
    )


def cost():
    return pl.CostEstimate(flops=1, bytes_accessed=1, transcendentals=0)


def spread(rows_of):
    return jnp.concatenate(
        [jnp.broadcast_to(rows_of[i : i + 1], (ROWS, rows_of.shape[1])) for i in range(GROUP)], axis=0
    )


def routing(route_ref, first):
    top, toks = route_ref.shape
    route = route_ref[...]
    ids = lax.broadcasted_iota(jnp.int32, (GROUP, toks), 0) + first
    hits = [jnp.broadcast_to(route[k : k + 1], (GROUP, toks)) == ids for k in range(top)]
    named = sum(h.astype(F32) for h in hits)
    return named, hits


def selection(named):
    toks = named.shape[1]
    before = (
        lax.broadcasted_iota(jnp.int32, (toks, toks), 0)
        < lax.broadcasted_iota(jnp.int32, (toks, toks), 1)
    ).astype(BF16)
    slot = dot(named.astype(BF16), before)
    code = jnp.where(named > 0, slot, -100.0)
    code = jnp.concatenate([code, code + float(SLOTS)], axis=1)
    place = lax.broadcasted_iota(jnp.int32, (ROWS, 2 * toks), 0).astype(F32)
    place = jnp.concatenate([place] * GROUP, axis=0)
    return spread(code) == place


def probs_of(hits, probs_ref):
    probs = probs_ref[...]
    chosen = sum(
        jnp.where(h, jnp.broadcast_to(probs[k : k + 1], h.shape), 0.0) for k, h in enumerate(hits)
    )
    return spread(jnp.concatenate([chosen, chosen], axis=1))


def stacked(x):
    half = x.shape[1] // 2
    return jnp.concatenate([x[:, :half], x[:, half:]], axis=0)


def send_kernel(scaled, route_ref, probs_ref, rows_ref, out_ref):
    named, hits = routing(route_ref, pl.program_id(0) * GROUP)
    sel = selection(named)
    picked = dot(sel.astype(F32).astype(BF16), stacked(rows_ref[...]))
    if scaled:
        weight = jnp.sum(jnp.where(sel, probs_of(hits, probs_ref), 0.0), axis=1, keepdims=True)
        picked = picked * weight
    out_ref[...] = picked.astype(BF16)


def send_rows(scaled, route_t, probs_t, rows, experts):
    toks, width = rows.shape
    top = route_t.shape[0]
    half = width // 2
    return pl.pallas_call(
        functools.partial(send_kernel, scaled),
        grid=(experts // GROUP,),
        in_specs=[
            pl.BlockSpec((top, toks), lambda i: (0, 0)),
            pl.BlockSpec((top, toks), lambda i: (0, 0)),
            pl.BlockSpec((toks, width), lambda i: (0, 0)),
        ],
        out_specs=pl.BlockSpec((TILE, half), lambda i: (i, 0)),
        out_shape=jax.ShapeDtypeStruct((experts * ROWS, half), BF16),
        compiler_params=params(60),
        cost_estimate=cost(),
        name="send_scaled" if scaled else "send_tokens",
    )(route_t, probs_t, rows)


SUB = 8


def ordering(back=False):
    n = SUB * ROWS
    row = lax.broadcasted_iota(jnp.int32, (n, n), int(back))
    col = lax.broadcasted_iota(jnp.int32, (n, n), 1 - int(back))
    upper = (row >= n // 2).astype(jnp.int32)
    within = row - upper * (n // 2)
    source = (within * 43) >> 9
    return (col == SLOTS * source + SLOTS * upper + within).astype(F32).astype(BF16)


def put_in_order(own_ref, other_ref, mine, step, held, out_ref):
    order = ordering()
    n = SUB * ROWS
    for which, ref in ((mine, own_ref), (1 - mine, other_ref)):
        for b in range(GROUP // SUB):
            both = dot(order, ref[b * n : (b + 1) * n, :]).astype(BF16)
            at = pl.multiple_of(step * (GROUP * SLOTS) + b * (n // 2), n // 2)
            for h in range(2):
                part = both[h * (n // 2) : (h + 1) * (n // 2)]
                held[2 * which + h, pl.ds(at, n // 2), :] = part
                out_ref[2 * which + h, b * (n // 2) : (b + 1) * (n // 2), :] = part


def weight_copies(gate_hbm, up_hbm, down_hbm, gate_w, up_w, down_w, sems):
    quarter = down_w.shape[2]
    downs = [
        pltpu.make_async_copy(
            down_hbm.at[:, q * quarter : (q + 1) * quarter], down_w.at[q], sems.at[2 + q]
        )
        for q in range(4)
    ]
    gates = pltpu.make_async_copy(gate_hbm, gate_w, sems.at[0])
    ups = pltpu.make_async_copy(up_hbm, up_w, sems.at[1])
    return [gates, ups], downs


def forward_kernel(
    steps, ff_steps, mine_ref, own_ref, other_ref, gate_hbm, up_hbm, down_hbm,
    gate_ref, up_ref, hidden_ref, rows_ref, far0, far1, near_ref,
    held, hidden_all, gate_w, up_w, down_w, sems,
):
    i = pl.program_id(0)
    mine = mine_ref[0]
    quarter = own_ref.shape[1]
    ins, downs = weight_copies(gate_hbm, up_hbm, down_hbm, gate_w, up_w, down_w, sems)

    @pl.when(i == 0)
    def _():
        for copy in ins + downs:
            copy.start()

    @pl.when(i < steps)
    def _():
        put_in_order(own_ref, other_ref, mine, i, held, rows_ref)

    for f in range(ff_steps):
        @pl.when(i == steps + f)
        def _():
            if f == 0:
                for copy in ins:
                    copy.wait()
            wide = gate_ref.shape[1]
            at = slice(f * wide, (f + 1) * wide)
            gate = sum(dot(held[q], gate_w[q * quarter : (q + 1) * quarter, at]) for q in range(4))
            up = sum(dot(held[q], up_w[q * quarter : (q + 1) * quarter, at]) for q in range(4))
            gate_ref[...] = gate
            up_ref[...] = up
            hidden = (gate * jax.nn.sigmoid(gate) * up).astype(BF16)
            hidden_ref[...] = hidden
            hidden_all[:, at] = hidden

    for h, far_ref in enumerate((far0, far1)):
        @pl.when(i == steps + ff_steps + h)
        def _():
            if h == 0:
                for copy in downs:
                    copy.wait()
            far_ref[...] = dot(hidden_all[...], down_w[2 * (1 - mine) + h]).astype(BF16)

    for h in range(2):
        @pl.when(i == steps + ff_steps + 2 + h)
        def _():
            near_ref[...] = dot(hidden_all[...], down_w[2 * mine + h]).astype(BF16)


def expert_specs(raw, quarter, ff, model):
    steps, ff_steps, rows = raw // TILE, 2, raw // 2
    wide = ff // ff_steps
    last = steps + ff_steps
    source = pl.BlockSpec((TILE, quarter), lambda i, m: (jnp.minimum(i, steps - 1), 0))
    ffs = pl.BlockSpec((rows, wide), lambda i, m: (0, jnp.clip(i - steps, 0, ff_steps - 1)))
    ordered = pl.BlockSpec(
        (4, GROUP * SLOTS, quarter), lambda i, m: (0, jnp.minimum(i, steps - 1), 0)
    )
    far = pl.BlockSpec((rows, quarter), lambda i, m: (0, 0))
    near = pl.BlockSpec((rows, quarter), lambda i, m: (0, jnp.clip(i - last - 2, 0, 1)))
    held = [
        pltpu.VMEM((model, ff), BF16),
        pltpu.VMEM((model, ff), BF16),
        pltpu.VMEM((4, ff, quarter), BF16),
        pltpu.SemaphoreType.DMA((6,)),
    ]
    return steps, ff_steps, rows, source, ffs, ordered, far, near, held


def forward(mine, own, other, gate_w, up_w, down_w):
    raw, quarter = own.shape
    model, ff = gate_w.shape
    steps, ff_steps, rows, source, ffs, ordered, far, near, held = expert_specs(
        raw, quarter, ff, model
    )
    hbm = pl.BlockSpec(memory_space=pl.ANY)
    return pl.pallas_call(
        functools.partial(forward_kernel, steps, ff_steps),
        grid_spec=pltpu.PrefetchScalarGridSpec(
            num_scalar_prefetch=1,
            grid=(steps + ff_steps + 4,),
            in_specs=[source, source, hbm, hbm, hbm],
            out_specs=[ffs, ffs, ffs, ordered, far, far, near],
            scratch_shapes=[
                pltpu.VMEM((4, rows, quarter), BF16), pltpu.VMEM((rows, ff), BF16), *held
            ],
        ),
        out_shape=[
            jax.ShapeDtypeStruct((rows, ff), F32),
            jax.ShapeDtypeStruct((rows, ff), F32),
            jax.ShapeDtypeStruct((rows, ff), BF16),
            jax.ShapeDtypeStruct((4, rows, quarter), BF16),
            jax.ShapeDtypeStruct((rows, quarter), BF16),
            jax.ShapeDtypeStruct((rows, quarter), BF16),
            jax.ShapeDtypeStruct((rows, 2 * quarter), BF16),
        ],
        compiler_params=params(60),
        cost_estimate=cost(),
        name="expert_forward",
    )(mine, own, other, gate_w, up_w, down_w)


def backward_kernel(
    steps, ff_steps, mine_ref, own_ref, other_ref, gate_hbm, up_hbm, down_hbm, gate_ref, up_ref,
    gate_grad_ref, up_grad_ref, rows_ref, far0, far1, near_ref,
    held, gate_grads, up_grads, gate_w, up_w, down_w, sems,
):
    i = pl.program_id(0)
    mine = mine_ref[0]
    quarter = own_ref.shape[1]
    ins, downs = weight_copies(gate_hbm, up_hbm, down_hbm, gate_w, up_w, down_w, sems)

    @pl.when(i == 0)
    def _():
        for copy in downs + ins:
            copy.start()

    @pl.when(i < steps)
    def _():
        put_in_order(own_ref, other_ref, mine, i, held, rows_ref)

    for f in range(ff_steps):
        @pl.when(i == steps + f)
        def _():
            if f == 0:
                for copy in downs:
                    copy.wait()
            wide = gate_ref.shape[1]
            at = slice(f * wide, (f + 1) * wide)
            hidden_grad = sum(dot(held[q], down_w[q, at, :], NT) for q in range(4))
            gate, up = gate_ref[...], up_ref[...]
            logistic = jax.nn.sigmoid(gate)
            gate_grad = (hidden_grad * up * logistic * (1.0 + gate * (1.0 - logistic))).astype(BF16)
            up_grad = (hidden_grad * (gate * logistic)).astype(BF16)
            gate_grad_ref[...] = gate_grad
            up_grad_ref[...] = up_grad
            gate_grads[:, at] = gate_grad
            up_grads[:, at] = up_grad

    def input_grads(q):
        at = pl.ds(pl.multiple_of(q * quarter, quarter), quarter)
        return (
            dot(gate_grads[...], gate_w[at, :], NT) + dot(up_grads[...], up_w[at, :], NT)
        ).astype(BF16)

    for h, far_ref in enumerate((far0, far1)):
        @pl.when(i == steps + ff_steps + h)
        def _():
            if h == 0:
                for copy in ins:
                    copy.wait()
            far_ref[...] = input_grads(2 * (1 - mine) + h)

    for h in range(2):
        @pl.when(i == steps + ff_steps + 2 + h)
        def _():
            near_ref[...] = input_grads(2 * mine + h)


def backward(mine, own, other, gate_w, up_w, down_w, gate_pre, up_pre):
    raw, quarter = own.shape
    model, ff = gate_w.shape
    steps, ff_steps, rows, source, ffs, ordered, far, near, held = expert_specs(
        raw, quarter, ff, model
    )
    hbm = pl.BlockSpec(memory_space=pl.ANY)
    return pl.pallas_call(
        functools.partial(backward_kernel, steps, ff_steps),
        grid_spec=pltpu.PrefetchScalarGridSpec(
            num_scalar_prefetch=1,
            grid=(steps + ff_steps + 4,),
            in_specs=[source, source, hbm, hbm, hbm, ffs, ffs],
            out_specs=[ffs, ffs, ordered, far, far, near],
            scratch_shapes=[
                pltpu.VMEM((4, rows, quarter), BF16),
                pltpu.VMEM((rows, ff), BF16),
                pltpu.VMEM((rows, ff), BF16),
                *held,
            ],
        ),
        out_shape=[
            jax.ShapeDtypeStruct((rows, ff), BF16),
            jax.ShapeDtypeStruct((rows, ff), BF16),
            jax.ShapeDtypeStruct((4, rows, quarter), BF16),
            jax.ShapeDtypeStruct((rows, quarter), BF16),
            jax.ShapeDtypeStruct((rows, quarter), BF16),
            jax.ShapeDtypeStruct((rows, 2 * quarter), BF16),
        ],
        compiler_params=params(60),
        cost_estimate=cost(),
        name="expert_backward",
    )(mine, own, other, gate_w, up_w, down_w, gate_pre, up_pre)


def pack_kernel(near_ref, far0, far1, out_ref):
    order = ordering(back=True)
    n = SUB * ROWS
    quarter = out_ref.shape[1]
    for b in range(GROUP // SUB):
        at = slice(b * (n // 2), (b + 1) * (n // 2))
        both = jnp.concatenate(
            [
                (
                    near_ref[at, h * quarter : (h + 1) * quarter].astype(F32)
                    + far[at, :].astype(F32)
                ).astype(BF16)
                for h, far in enumerate((far0, far1))
            ],
            axis=0,
        )
        out_ref[b * n : (b + 1) * n, :] = dot(order, both).astype(BF16)


def pack(near, fars):
    rows, width = near.shape
    step_rows = GROUP * SLOTS
    return pl.pallas_call(
        pack_kernel,
        grid=(rows // step_rows,),
        in_specs=[
            pl.BlockSpec((step_rows, width), lambda i: (i, 0)),
            pl.BlockSpec((step_rows, width // 2), lambda i: (i, 0)),
            pl.BlockSpec((step_rows, width // 2), lambda i: (i, 0)),
        ],
        out_specs=pl.BlockSpec((TILE, width // 2), lambda i: (i, 0)),
        out_shape=jax.ShapeDtypeStruct((2 * rows, width // 2), BF16),
        compiler_params=params(48),
        cost_estimate=cost(),
        name="pack",
    )(near, *fars)


def weights_kernel(rows_ref, scaled_ref, hidden_ref, gate_grad_ref, up_grad_ref, gate_w, up_w, down_w):
    rows = rows_ref[0]
    gate_w[...] = dot(rows, gate_grad_ref[...], TN).astype(BF16)
    up_w[...] = dot(rows, up_grad_ref[...], TN).astype(BF16)
    down_w[...] = dot(hidden_ref[...], scaled_ref[0], TN).astype(BF16)


def weight_grads(token_rows, scaled_rows, hidden, gate_grad, up_grad):
    quarters, rows, quarter = token_rows.shape
    ff = hidden.shape[1]
    whole = pl.BlockSpec((rows, ff), lambda i: (0, 0))
    part = pl.BlockSpec((1, rows, quarter), lambda i: (i, 0, 0))
    return pl.pallas_call(
        weights_kernel,
        grid=(quarters,),
        in_specs=[part, part, whole, whole, whole],
        out_specs=[
            pl.BlockSpec((quarter, ff), lambda i: (i, 0)),
            pl.BlockSpec((quarter, ff), lambda i: (i, 0)),
            pl.BlockSpec((ff, quarter), lambda i: (0, i)),
        ],
        out_shape=[
            jax.ShapeDtypeStruct((quarters * quarter, ff), BF16),
            jax.ShapeDtypeStruct((quarters * quarter, ff), BF16),
            jax.ShapeDtypeStruct((ff, quarters * quarter), BF16),
        ],
        compiler_params=params(60),
        cost_estimate=cost(),
        name="weight_grads",
    )(token_rows, scaled_rows, hidden, gate_grad, up_grad)


def outputs_kernel(route_ref, probs_ref, cot_ref, back_ref, out_ref, grad_ref, sel_ref, total):
    i = pl.program_id(0)

    @pl.when(i == 0)
    def _():
        total[...] = jnp.zeros_like(total)
        grad_ref[...] = jnp.zeros_like(grad_ref)

    toks = cot_ref.shape[0]
    half = back_ref.shape[1]
    named, hits = routing(route_ref, i * GROUP)
    sel = selection(named)
    sel_ref[...] = sel.astype(F32).T.astype(BF16)
    weight = jnp.where(sel, probs_of(hits, probs_ref), 0.0)
    high = weight.astype(BF16)
    low = (weight - high.astype(F32)).astype(BF16)
    back = back_ref[...]
    total[...] += dot(high, back, TN) + dot(low, back, TN)
    products = jnp.where(sel, dot(back, stacked(cot_ref[...]), NT), 0.0)
    sums = jnp.concatenate(
        [
            jnp.sum(products[e * ROWS : (e + 1) * ROWS], axis=0, keepdims=True)
            for e in range(GROUP)
        ],
        axis=0,
    )
    sums = sums[:, :toks] + sums[:, toks:]
    grad_ref[...] += jnp.concatenate(
        [jnp.sum(jnp.where(h, sums, 0.0), axis=0, keepdims=True) for h in hits], axis=0
    )

    @pl.when(i == pl.num_programs(0) - 1)
    def _():
        out_ref[:, :half] = total[:toks].astype(BF16)
        out_ref[:, half:] = total[toks:].astype(BF16)


def token_outputs(route_t, probs_t, cot, back):
    toks, width = cot.shape
    top = route_t.shape[0]
    steps = back.shape[0] // TILE
    small = pl.BlockSpec((top, toks), lambda i: (0, 0))
    wide = pl.BlockSpec((toks, width), lambda i: (0, 0))
    return pl.pallas_call(
        outputs_kernel,
        grid=(steps,),
        in_specs=[small, small, wide, pl.BlockSpec((TILE, width // 2), lambda i: (i, 0))],
        out_specs=[wide, small, pl.BlockSpec((2 * toks, TILE), lambda i: (0, i))],
        out_shape=[
            jax.ShapeDtypeStruct((toks, width), BF16),
            jax.ShapeDtypeStruct((top, toks), F32),
            jax.ShapeDtypeStruct((2 * toks, back.shape[0]), BF16),
        ],
        scratch_shapes=[pltpu.VMEM((2 * toks, width // 2), F32)],
        compiler_params=params(60),
        cost_estimate=cost(),
        name="token_outputs",
    )(route_t, probs_t, cot, back)


def inputs_kernel(sel_ref, back_ref, out_ref, total):
    i = pl.program_id(0)
    toks, width = out_ref.shape
    half = width // 2
    part = dot(sel_ref[...], back_ref[...])

    @pl.when(i == 0)
    def _():
        total[...] = part

    @pl.when(i > 0)
    def _():
        total[...] += part

    @pl.when(i == pl.num_programs(0) - 1)
    def _():
        out_ref[:, :half] = total[:toks].astype(BF16)
        out_ref[:, half:] = total[toks:].astype(BF16)


def token_grads(select, back):
    raw, half = back.shape
    toks = select.shape[0] // 2
    return pl.pallas_call(
        inputs_kernel,
        grid=(2,),
        in_specs=[
            pl.BlockSpec((2 * toks, raw // 2), lambda i: (0, i)),
            pl.BlockSpec((raw // 2, half), lambda i: (i, 0)),
        ],
        out_specs=pl.BlockSpec((toks, 2 * half), lambda i: (0, 0)),
        out_shape=jax.ShapeDtypeStruct((toks, 2 * half), BF16),
        scratch_shapes=[pltpu.VMEM((2 * toks, half), F32)],
        compiler_params=params(60),
        cost_estimate=cost(),
        name="token_grads",
    )(select, back)


def exchange(x):
    experts = lax.axis_size("expert")
    y = lax.all_to_all(
        x.reshape(experts, ROWS, -1), "expert", split_axis=0, concat_axis=0, tiled=True
    )
    return y.reshape(x.shape)


def swap(x):
    return lax.ppermute(x, "mp", [(0, 1), (1, 0)])


def body(tokens, cotangent, route_ids, gate_probs, w_gate, w_up, w_down):
    experts = lax.axis_size("expert")
    mine = lax.axis_index("mp").astype(jnp.int32).reshape(1)
    route_t, probs_t = route_ids.T, gate_probs.T
    gate_w, up_w, down_w = w_gate[0], w_up[0], w_down[0]

    send_tokens = send_rows(False, route_t, probs_t, tokens, experts)
    send_scaled = send_rows(True, route_t, probs_t, cotangent, experts)
    got_tokens, send_scaled = lax.optimization_barrier((exchange(send_tokens), send_scaled))
    got_scaled = exchange(send_scaled)

    gate_pre, up_pre, hidden, token_rows, far0, far1, out_near = forward(
        mine, got_tokens, swap(got_tokens), gate_w, up_w, down_w
    )
    send_out = pack(out_near, [swap(far0), swap(far1)])
    got_scaled, send_out = lax.optimization_barrier((got_scaled, send_out))
    back_out = exchange(send_out)

    gate_grad, up_grad, scaled_rows, far0, far1, in_near = backward(
        mine, got_scaled, swap(got_scaled), gate_w, up_w, down_w, gate_pre, up_pre
    )
    send_in = pack(in_near, [swap(far0), swap(far1)])
    back_out, send_in = lax.optimization_barrier((back_out, send_in))
    back_in = exchange(send_in)

    grad_w_gate, grad_w_up, grad_w_down = weight_grads(
        token_rows, scaled_rows, hidden, gate_grad, up_grad
    )
    layer_out, grad_part, select = token_outputs(route_t, probs_t, cotangent, back_out)
    grad_probs = lax.psum(grad_part, "mp").T
    grad_tokens = token_grads(select, back_in)
    return (
        layer_out, grad_tokens, grad_probs, grad_w_gate[None], grad_w_up[None], grad_w_down[None],
    )


def solution(mesh):
    return jax.shard_map(
        body,
        mesh=mesh,
        in_specs=(
            P("expert", "mp"),
            P("expert", "mp"),
            P("expert", None),
            P("expert", None),
            P("expert", None, "mp"),
            P("expert", None, "mp"),
            P("expert", "mp", None),
        ),
        out_specs=(
            P("expert", "mp"),
            P("expert", "mp"),
            P("expert", None),
            P("expert", None, "mp"),
            P("expert", None, "mp"),
            P("expert", "mp", None),
        ),
        check_vma=False,
    )
```

```python
import functools
import jax
import jax.numpy as jnp
from jax import lax
from jax.experimental import pallas as pl
from jax.experimental.pallas import tpu as pltpu
from jax.sharding import PartitionSpec as P

BF16 = jnp.bfloat16
F32 = jnp.float32
SLOTS = 12
ROWS = 2 * SLOTS
PLANES = 4
PLANE_ROWS = PLANES * SLOTS
GROUP = 16
TILE = GROUP * ROWS

NN = (((1,), (0,)), ((), ()))
NT = (((1,), (1,)), ((), ()))
TN = (((0,), (0,)), ((), ()))


def dot(a, b, dims=NN):
    return lax.dot_general(a, b, dims, preferred_element_type=F32)


def params(mebibytes):
    return pltpu.CompilerParams(
        vmem_limit_bytes=mebibytes * 1024 * 1024, dimension_semantics=("arbitrary",)
    )


def cost():
    return pl.CostEstimate(flops=1, bytes_accessed=1, transcendentals=0)


def spread(rows_of):
    return jnp.concatenate(
        [jnp.broadcast_to(rows_of[i : i + 1], (ROWS, rows_of.shape[1])) for i in range(GROUP)], axis=0
    )


def routing(route_ref, first):
    top, toks = route_ref.shape
    route = route_ref[...]
    ids = lax.broadcasted_iota(jnp.int32, (GROUP, toks), 0) + first
    hits = [jnp.broadcast_to(route[k : k + 1], (GROUP, toks)) == ids for k in range(top)]
    named = sum(h.astype(F32) for h in hits)
    return named, hits


def selection(named):
    toks = named.shape[1]
    before = (
        lax.broadcasted_iota(jnp.int32, (toks, toks), 0)
        < lax.broadcasted_iota(jnp.int32, (toks, toks), 1)
    ).astype(BF16)
    slot = dot(named.astype(BF16), before)
    code = jnp.where(named > 0, slot, -100.0)
    code = jnp.concatenate([code, code + float(SLOTS)], axis=1)
    place = lax.broadcasted_iota(jnp.int32, (ROWS, 2 * toks), 0).astype(F32)
    place = jnp.concatenate([place] * GROUP, axis=0)
    return spread(code) == place


def plane_selection(info_ref, first, count):
    info = info_ref[...]
    top, toks = info.shape[0] // 2, info.shape[1]
    each = toks // PLANES
    ids = (lax.broadcasted_iota(jnp.int32, (count, toks), 0) + first).astype(F32)
    hits = [jnp.broadcast_to(info[k : k + 1], (count, toks)) == ids for k in range(top)]
    named = sum(h.astype(F32) for h in hits)
    chosen = sum(
        jnp.where(h, jnp.broadcast_to(info[top + k : top + k + 1], h.shape), 0.0)
        for k, h in enumerate(hits)
    )
    row = lax.broadcasted_iota(jnp.int32, (toks, toks), 0)
    col = lax.broadcasted_iota(jnp.int32, (toks, toks), 1)
    shift = each.bit_length() - 1
    before = jnp.logical_and(row < col, (row >> shift) == (col >> shift)).astype(F32).astype(BF16)
    chip = (lax.broadcasted_iota(jnp.int32, (count, toks), 1) >> shift).astype(F32)
    code = jnp.where(named > 0, dot(named.astype(BF16), before) + SLOTS * chip, -100.0)

    def widen(x):
        return jnp.concatenate(
            [jnp.broadcast_to(x[e : e + 1], (PLANE_ROWS, toks)) for e in range(count)], axis=0
        )

    place = lax.broadcasted_iota(jnp.int32, (PLANE_ROWS, toks), 0).astype(F32)
    sel = widen(code) == jnp.concatenate([place] * count, axis=0)
    return sel, hits, jnp.where(sel, widen(chosen), 0.0)


def column(refs, h):
    half = refs[0].shape[1] // 2
    return jnp.concatenate([ref[:, h * half : (h + 1) * half] for ref in refs], axis=0)


def plane_send_kernel(first_ref, info_ref, rows0, rows1, rows2, rows3, out_ref):
    count = out_ref.shape[0]
    sel, _, weights = plane_selection(info_ref, first_ref[0] + pl.program_id(0) * count, count)
    weight = jnp.sum(weights, axis=1, keepdims=True)
    take = sel.astype(F32).astype(BF16)
    for h in range(2):
        picked = (dot(take, column((rows0, rows1, rows2, rows3), h)) * weight).astype(BF16)
        out_ref[:, h * PLANE_ROWS : (h + 1) * PLANE_ROWS, :] = picked.reshape(
            count, PLANE_ROWS, picked.shape[1]
        )


PLANE_STEP = 4


def plane_send(first, info, pieces, experts):
    toks, width = pieces[0].shape
    whole = lambda i, m: (0, 0)
    return pl.pallas_call(
        plane_send_kernel,
        grid_spec=pltpu.PrefetchScalarGridSpec(
            num_scalar_prefetch=1,
            grid=(experts // PLANE_STEP,),
            in_specs=[pl.BlockSpec(info.shape, whole)]
            + [pl.BlockSpec((toks, width), whole)] * PLANES,
            out_specs=pl.BlockSpec(
                (PLANE_STEP, 2 * PLANE_ROWS, width // 2), lambda i, m: (i, 0, 0)
            ),
        ),
        out_shape=jax.ShapeDtypeStruct((experts, 2 * PLANE_ROWS, width // 2), BF16),
        compiler_params=params(60),
        cost_estimate=cost(),
        name="send_scaled",
    )(first, info, *pieces)


def stacked(x):
    half = x.shape[1] // 2
    return jnp.concatenate([x[:, :half], x[:, half:]], axis=0)


def send_kernel(route_ref, rows_ref, out_ref):
    named, _ = routing(route_ref, pl.program_id(0) * GROUP)
    sel = selection(named).astype(F32).astype(BF16)
    out_ref[...] = dot(sel, stacked(rows_ref[...])).astype(BF16)


def send_rows(route_t, rows, experts):
    toks, width = rows.shape
    top = route_t.shape[0]
    half = width // 2
    return pl.pallas_call(
        send_kernel,
        grid=(experts // GROUP,),
        in_specs=[
            pl.BlockSpec((top, toks), lambda i: (0, 0)),
            pl.BlockSpec((toks, width), lambda i: (0, 0)),
        ],
        out_specs=pl.BlockSpec((TILE, half), lambda i: (i, 0)),
        out_shape=jax.ShapeDtypeStruct((experts * ROWS, half), BF16),
        compiler_params=params(60),
        cost_estimate=cost(),
        name="send_tokens",
    )(route_t, rows)


def select_kernel(route_ref, out_ref):
    named, _ = routing(route_ref, pl.program_id(0) * GROUP)
    out_ref[...] = selection(named).astype(F32).T.astype(BF16)


def select_rows(route_t, experts):
    top, toks = route_t.shape
    return pl.pallas_call(
        select_kernel,
        grid=(experts // GROUP,),
        in_specs=[pl.BlockSpec((top, toks), lambda i: (0, 0))],
        out_specs=pl.BlockSpec((2 * toks, TILE), lambda i: (0, i)),
        out_shape=jax.ShapeDtypeStruct((2 * toks, experts * ROWS), BF16),
        compiler_params=params(60),
        cost_estimate=cost(),
        name="select_rows",
    )(route_t)


COLUMNS = 2
ORDERED = COLUMNS * PLANE_ROWS


def ordering(back=False):
    n = 2 * ORDERED
    row = lax.broadcasted_iota(jnp.int32, (n, n), int(back))
    col = lax.broadcasted_iota(jnp.int32, (n, n), 1 - int(back))
    upper = (row >= ORDERED).astype(jnp.int32)
    within = row - upper * ORDERED
    second = (within >= PLANE_ROWS).astype(jnp.int32)
    within = within - second * PLANE_ROWS
    chip = (within * 43) >> 9
    target = chip * (COLUMNS * ROWS) + second * ROWS + upper * SLOTS + within - SLOTS * chip
    return (col == target).astype(F32).astype(BF16)


def plane_of(r, plane):
    return lax.rem(plane + PLANES - r, PLANES)


def put_in_order(own_ref, other_ref, mine, plane, step, held, out_ref):
    order = ordering()
    n = COLUMNS * ROWS
    for which, ref in ((mine, own_ref), (1 - mine, other_ref)):
        for b in range(ref.shape[1] // n):
            raw = jnp.concatenate(
                [ref[plane_of(r, plane), b * n : (b + 1) * n, :] for r in range(PLANES)], axis=0
            )
            both = dot(order, raw).astype(BF16)
            at = pl.multiple_of(step * (GROUP * SLOTS) + b * ORDERED, ORDERED)
            for h in range(2):
                part = both[h * ORDERED : (h + 1) * ORDERED]
                held[2 * which + h, pl.ds(at, ORDERED), :] = part
                out_ref[2 * which + h, b * ORDERED : (b + 1) * ORDERED, :] = part


def weight_copies(gate_hbm, up_hbm, down_hbm, gate_w, up_w, down_w, sems):
    quarter = down_w.shape[2]
    downs = [
        pltpu.make_async_copy(
            down_hbm.at[:, q * quarter : (q + 1) * quarter], down_w.at[q], sems.at[2 + q]
        )
        for q in range(4)
    ]
    gates = pltpu.make_async_copy(gate_hbm, gate_w, sems.at[0])
    ups = pltpu.make_async_copy(up_hbm, up_w, sems.at[1])
    return [gates, ups], downs


def forward_kernel(
    steps, ff_steps, mine_ref, own_ref, other_ref, gate_hbm, up_hbm, down_hbm,
    gate_ref, up_ref, hidden_ref, rows_ref, far0, far1, near_ref,
    held, hidden_all, gate_w, up_w, down_w, sems,
):
    i = pl.program_id(0)
    mine, plane = mine_ref[0], mine_ref[1]
    quarter = own_ref.shape[2]
    ins, downs = weight_copies(gate_hbm, up_hbm, down_hbm, gate_w, up_w, down_w, sems)

    @pl.when(i == 0)
    def _():
        for copy in ins + downs:
            copy.start()

    @pl.when(i < steps)
    def _():
        put_in_order(own_ref, other_ref, mine, plane, i, held, rows_ref)

    for f in range(ff_steps):
        @pl.when(i == steps + f)
        def _():
            if f == 0:
                for copy in ins:
                    copy.wait()
            wide = gate_ref.shape[1]
            at = slice(f * wide, (f + 1) * wide)
            gate = sum(dot(held[q], gate_w[q * quarter : (q + 1) * quarter, at]) for q in range(4))
            up = sum(dot(held[q], up_w[q * quarter : (q + 1) * quarter, at]) for q in range(4))
            gate_ref[...] = gate
            up_ref[...] = up
            hidden = (gate * jax.nn.sigmoid(gate) * up).astype(BF16)
            hidden_ref[...] = hidden
            hidden_all[:, at] = hidden

    for h, far_ref in enumerate((far0, far1)):
        @pl.when(i == steps + ff_steps + h)
        def _():
            if h == 0:
                for copy in downs:
                    copy.wait()
            part = dot(hidden_all[...], down_w[2 * (1 - mine) + h]).astype(BF16)
            far_ref[...] = part.reshape(far_ref.shape)

    for h in range(2):
        @pl.when(i == steps + ff_steps + 2 + h)
        def _():
            part = dot(hidden_all[...], down_w[2 * mine + h]).astype(BF16)
            near_ref[...] = part.reshape(near_ref.shape)


def weight_scratch(model, ff):
    return [
        pltpu.VMEM((model, ff), BF16),
        pltpu.VMEM((model, ff), BF16),
        pltpu.VMEM((4, ff, model // 4), BF16),
        pltpu.SemaphoreType.DMA((6,)),
    ]


def forward(mine, own, other, gate_w, up_w, down_w):
    raw, quarter = own.shape
    model, ff = gate_w.shape
    rows, ff_steps, columns = raw // 2, 2, raw // (2 * PLANE_ROWS)
    steps = raw // TILE
    last = steps + ff_steps
    source = pl.BlockSpec(
        (PLANES, TILE // PLANES, quarter), lambda i, m: (0, jnp.minimum(i, steps - 1), 0)
    )
    ffs = pl.BlockSpec(
        (rows, ff // ff_steps), lambda i, m: (0, jnp.clip(i - steps, 0, ff_steps - 1))
    )
    ordered = pl.BlockSpec(
        (4, GROUP * SLOTS, quarter), lambda i, m: (0, jnp.minimum(i, steps - 1), 0)
    )
    far = pl.BlockSpec((columns, PLANE_ROWS, quarter), lambda i, m: (0, 0, 0))
    near = pl.BlockSpec(
        (columns, PLANE_ROWS, quarter), lambda i, m: (0, jnp.clip(i - last - 2, 0, 1), 0)
    )
    hbm = pl.BlockSpec(memory_space=pl.ANY)
    by_plane = (PLANES, raw // PLANES, quarter)
    return pl.pallas_call(
        functools.partial(forward_kernel, steps, ff_steps),
        grid_spec=pltpu.PrefetchScalarGridSpec(
            num_scalar_prefetch=1,
            grid=(last + 4,),
            in_specs=[source, source, hbm, hbm, hbm],
            out_specs=[ffs, ffs, ffs, ordered, far, far, near],
            scratch_shapes=[
                pltpu.VMEM((4, rows, quarter), BF16),
                pltpu.VMEM((rows, ff), BF16),
                *weight_scratch(model, ff),
            ],
        ),
        out_shape=[
            jax.ShapeDtypeStruct((rows, ff), F32),
            jax.ShapeDtypeStruct((rows, ff), F32),
            jax.ShapeDtypeStruct((rows, ff), BF16),
            jax.ShapeDtypeStruct((4, rows, quarter), BF16),
            jax.ShapeDtypeStruct((columns, PLANE_ROWS, quarter), BF16),
            jax.ShapeDtypeStruct((columns, PLANE_ROWS, quarter), BF16),
            jax.ShapeDtypeStruct((columns, 2 * PLANE_ROWS, quarter), BF16),
        ],
        compiler_params=params(60),
        cost_estimate=cost(),
        name="expert_forward",
    )(mine, own.reshape(by_plane), other.reshape(by_plane), gate_w, up_w, down_w)


def backward_kernel(
    ff_steps, mine_ref, own0, own1, other0, other1, gate_hbm, up_hbm, down_hbm, gate_ref, up_ref,
    gate_grad_ref, up_grad_ref, far0, far1, near_ref,
    gate_grads, up_grads, gate_w, up_w, down_w, sems,
):
    i = pl.program_id(0)
    mine = mine_ref[0]
    rows, quarter = far0.shape
    ins, downs = weight_copies(gate_hbm, up_hbm, down_hbm, gate_w, up_w, down_w, sems)

    @pl.when(i == 0)
    def _():
        for copy in downs + ins:
            copy.start()

    for f in range(ff_steps):
        @pl.when(i == f)
        def _():
            if f == 0:
                for copy in downs:
                    copy.wait()
            wide = gate_ref.shape[1]
            at = slice(f * wide, (f + 1) * wide)
            hidden_grad = sum(
                dot(ref[...].reshape(rows, quarter), down_w[q, at, :], NT)
                for q, ref in (
                    (2 * mine, own0),
                    (2 * mine + 1, own1),
                    (2 * (1 - mine), other0),
                    (2 * (1 - mine) + 1, other1),
                )
            )
            gate, up = gate_ref[...], up_ref[...]
            logistic = jax.nn.sigmoid(gate)
            gate_grad = (hidden_grad * up * logistic * (1.0 + gate * (1.0 - logistic))).astype(BF16)
            up_grad = (hidden_grad * (gate * logistic)).astype(BF16)
            gate_grad_ref[...] = gate_grad
            up_grad_ref[...] = up_grad
            gate_grads[:, at] = gate_grad
            up_grads[:, at] = up_grad

    def input_grads(q):
        at = pl.ds(pl.multiple_of(q * quarter, quarter), quarter)
        return (
            dot(gate_grads[...], gate_w[at, :], NT) + dot(up_grads[...], up_w[at, :], NT)
        ).astype(BF16)

    for h, far_ref in enumerate((far0, far1)):
        @pl.when(i == ff_steps + h)
        def _():
            if h == 0:
                for copy in ins:
                    copy.wait()
            far_ref[...] = input_grads(2 * (1 - mine) + h)

    for h in range(2):
        @pl.when(i == ff_steps + 2 + h)
        def _():
            near_ref[...] = input_grads(2 * mine + h)


def backward(mine, own, other, gate_w, up_w, down_w, gate_pre, up_pre):
    columns, _, quarter = own.shape
    model, ff = gate_w.shape
    rows, ff_steps = columns * PLANE_ROWS, 2
    halves = [
        pl.BlockSpec((columns, PLANE_ROWS, quarter), lambda i, m, h=h: (0, h, 0)) for h in range(2)
    ]
    ffs = pl.BlockSpec((rows, ff // ff_steps), lambda i, m: (0, jnp.clip(i, 0, ff_steps - 1)))
    far = pl.BlockSpec((rows, quarter), lambda i, m: (0, 0))
    near = pl.BlockSpec((rows, quarter), lambda i, m: (0, jnp.clip(i - ff_steps - 2, 0, 1)))
    hbm = pl.BlockSpec(memory_space=pl.ANY)
    return pl.pallas_call(
        functools.partial(backward_kernel, ff_steps),
        grid_spec=pltpu.PrefetchScalarGridSpec(
            num_scalar_prefetch=1,
            grid=(ff_steps + 4,),
            in_specs=[*halves, *halves, hbm, hbm, hbm, ffs, ffs],
            out_specs=[ffs, ffs, far, far, near],
            scratch_shapes=[
                pltpu.VMEM((rows, ff), BF16),
                pltpu.VMEM((rows, ff), BF16),
                *weight_scratch(model, ff),
            ],
        ),
        out_shape=[
            jax.ShapeDtypeStruct((rows, ff), BF16),
            jax.ShapeDtypeStruct((rows, ff), BF16),
            jax.ShapeDtypeStruct((rows, quarter), BF16),
            jax.ShapeDtypeStruct((rows, quarter), BF16),
            jax.ShapeDtypeStruct((rows, 2 * quarter), BF16),
        ],
        compiler_params=params(60),
        cost_estimate=cost(),
        name="expert_backward",
    )(mine, own, own, other, other, gate_w, up_w, down_w, gate_pre, up_pre)


def add_kernel(near_ref, far0, far1, out_ref):
    for h, far in enumerate((far0, far1)):
        at = slice(h * PLANE_ROWS, (h + 1) * PLANE_ROWS)
        out_ref[:, at, :] = (near_ref[:, at, :].astype(F32) + far[...].astype(F32)).astype(BF16)


def add_halves(near, fars):
    columns, both, quarter = near.shape
    step = columns // 4
    wide = pl.BlockSpec((step, both, quarter), lambda i: (i, 0, 0))
    half = pl.BlockSpec((step, both // 2, quarter), lambda i: (i, 0, 0))
    return pl.pallas_call(
        add_kernel,
        grid=(4,),
        in_specs=[wide, half, half],
        out_specs=wide,
        out_shape=jax.ShapeDtypeStruct(near.shape, BF16),
        compiler_params=params(48),
        cost_estimate=cost(),
        name="add_halves",
    )(near, *fars)


def pack_kernel(plane_ref, near_ref, far0, far1, out_ref):
    order = ordering(back=True)
    n = COLUMNS * ROWS
    quarter = out_ref.shape[2]
    plane = plane_ref[1]
    for b in range(out_ref.shape[1] // n):
        at = slice(b * ORDERED, (b + 1) * ORDERED)
        both = jnp.concatenate(
            [
                (
                    near_ref[at, h * quarter : (h + 1) * quarter].astype(F32)
                    + far[at, :].astype(F32)
                ).astype(BF16)
                for h, far in enumerate((far0, far1))
            ],
            axis=0,
        )
        raw = dot(order, both).astype(BF16)
        for r in range(PLANES):
            out_ref[plane_of(r, plane), b * n : (b + 1) * n, :] = raw[r * n : (r + 1) * n]


def pack(mine, near, fars):
    rows, width = near.shape
    step_rows = GROUP * SLOTS
    return pl.pallas_call(
        pack_kernel,
        grid_spec=pltpu.PrefetchScalarGridSpec(
            num_scalar_prefetch=1,
            grid=(rows // step_rows,),
            in_specs=[
                pl.BlockSpec((step_rows, width), lambda i, m: (i, 0)),
                pl.BlockSpec((step_rows, width // 2), lambda i, m: (i, 0)),
                pl.BlockSpec((step_rows, width // 2), lambda i, m: (i, 0)),
            ],
            out_specs=pl.BlockSpec(
                (PLANES, TILE // PLANES, width // 2), lambda i, m: (0, i, 0)
            ),
        ),
        out_shape=jax.ShapeDtypeStruct((PLANES, 2 * rows // PLANES, width // 2), BF16),
        compiler_params=params(48),
        cost_estimate=cost(),
        name="pack",
    )(mine, near, *fars).reshape(2 * rows, width // 2)


def weights_kernel(
    mine_ref, rows_ref, own_ref, other_ref, hidden_ref, gate_grad_ref, up_grad_ref,
    gate_w, up_w, down_w,
):
    rows = rows_ref[0]
    gate_w[...] = dot(rows, gate_grad_ref[...], TN).astype(BF16)
    up_w[...] = dot(rows, up_grad_ref[...], TN).astype(BF16)

    @pl.when(pl.program_id(0) < 2)
    def _():
        scaled = own_ref[...].reshape(rows.shape)
        down_w[...] = dot(hidden_ref[...], scaled, TN).astype(BF16)

    @pl.when(pl.program_id(0) >= 2)
    def _():
        scaled = other_ref[...].reshape(rows.shape)
        down_w[...] = dot(hidden_ref[...], scaled, TN).astype(BF16)


def weight_grads(mine, token_rows, own, other, hidden, gate_grad, up_grad):
    quarters, rows, quarter = token_rows.shape
    columns = own.shape[0]
    ff = hidden.shape[1]
    place = lambda i, m: lax.rem(2 * m[0] + i, 4)
    whole = pl.BlockSpec((rows, ff), lambda i, m: (0, 0))
    half = (columns, PLANE_ROWS, quarter)
    return pl.pallas_call(
        weights_kernel,
        grid_spec=pltpu.PrefetchScalarGridSpec(
            num_scalar_prefetch=1,
            grid=(quarters,),
            in_specs=[
                pl.BlockSpec((1, rows, quarter), lambda i, m: (place(i, m), 0, 0)),
                pl.BlockSpec(half, lambda i, m: (0, jnp.minimum(i, 1), 0)),
                pl.BlockSpec(half, lambda i, m: (0, jnp.maximum(i - 2, 0), 0)),
                whole, whole, whole,
            ],
            out_specs=[
                pl.BlockSpec((quarter, ff), lambda i, m: (place(i, m), 0)),
                pl.BlockSpec((quarter, ff), lambda i, m: (place(i, m), 0)),
                pl.BlockSpec((ff, quarter), lambda i, m: (0, place(i, m))),
            ],
        ),
        out_shape=[
            jax.ShapeDtypeStruct((quarters * quarter, ff), BF16),
            jax.ShapeDtypeStruct((quarters * quarter, ff), BF16),
            jax.ShapeDtypeStruct((ff, quarters * quarter), BF16),
        ],
        compiler_params=params(60),
        cost_estimate=cost(),
        name="weight_grads",
    )(mine, token_rows, own, other, hidden, gate_grad, up_grad)


def outputs_kernel(
    first_ref, info_ref, cot0, cot1, cot2, cot3, back_ref, out0, out1, out2, out3, grad_ref, total,
):
    i = pl.program_id(0)

    @pl.when(i == 0)
    def _():
        total[...] = jnp.zeros_like(total)
        grad_ref[...] = jnp.zeros_like(grad_ref)

    count, _, half = back_ref.shape
    toks = cot0.shape[0]
    sel, hits, weight = plane_selection(info_ref, first_ref[0] + i * count, count)
    high = weight.astype(BF16)
    low = (weight - high.astype(F32)).astype(BF16)
    products = 0.0
    for h in range(2):
        back = back_ref[:, h * PLANE_ROWS : (h + 1) * PLANE_ROWS, :].reshape(
            count * PLANE_ROWS, half
        )
        total[h] += dot(high, back, TN) + dot(low, back, TN)
        products += dot(back, column((cot0, cot1, cot2, cot3), h), NT)
    products = jnp.where(sel, products, 0.0)
    sums = jnp.concatenate(
        [
            jnp.sum(products[e * PLANE_ROWS : (e + 1) * PLANE_ROWS], axis=0, keepdims=True)
            for e in range(count)
        ],
        axis=0,
    )
    grad_ref[...] += jnp.concatenate(
        [jnp.sum(jnp.where(h, sums, 0.0), axis=0, keepdims=True) for h in hits], axis=0
    )

    @pl.when(i == pl.num_programs(0) - 1)
    def _():
        for r, ref in enumerate((out0, out1, out2, out3)):
            for h in range(2):
                ref[:, h * half : (h + 1) * half] = total[h, r * toks : (r + 1) * toks].astype(BF16)


def token_outputs(first, info, cots, back):
    toks, width = cots[0].shape
    experts, both, half = back.shape
    whole = lambda i, m: (0, 0)
    wide = pl.BlockSpec((toks, width), whole)
    grads = (info.shape[0] // 2, info.shape[1])
    return pl.pallas_call(
        outputs_kernel,
        grid_spec=pltpu.PrefetchScalarGridSpec(
            num_scalar_prefetch=1,
            grid=(experts // PLANE_STEP,),
            in_specs=[pl.BlockSpec(info.shape, whole)]
            + [wide] * PLANES
            + [pl.BlockSpec((PLANE_STEP, both, half), lambda i, m: (i, 0, 0))],
            out_specs=[wide] * PLANES + [pl.BlockSpec(grads, whole)],
            scratch_shapes=[pltpu.VMEM((2, PLANES * toks, half), F32)],
        ),
        out_shape=[jax.ShapeDtypeStruct((toks, width), BF16)] * PLANES
        + [jax.ShapeDtypeStruct(grads, F32)],
        compiler_params=params(60),
        cost_estimate=cost(),
        name="token_outputs",
    )(first, info, *cots, back)


def inputs_kernel(sel_ref, back_ref, out_ref, total):
    i = pl.program_id(0)
    toks, width = out_ref.shape
    half = width // 2
    part = dot(sel_ref[...], back_ref[...])

    @pl.when(i == 0)
    def _():
        total[...] = part

    @pl.when(i > 0)
    def _():
        total[...] += part

    @pl.when(i == pl.num_programs(0) - 1)
    def _():
        out_ref[:, :half] = total[:toks].astype(BF16)
        out_ref[:, half:] = total[toks:].astype(BF16)


def token_grads(select, back):
    raw, half = back.shape
    toks = select.shape[0] // 2
    return pl.pallas_call(
        inputs_kernel,
        grid=(2,),
        in_specs=[
            pl.BlockSpec((2 * toks, raw // 2), lambda i: (0, i)),
            pl.BlockSpec((raw // 2, half), lambda i: (i, 0)),
        ],
        out_specs=pl.BlockSpec((toks, 2 * half), lambda i: (0, 0)),
        out_shape=jax.ShapeDtypeStruct((toks, 2 * half), BF16),
        scratch_shapes=[pltpu.VMEM((2 * toks, half), F32)],
        compiler_params=params(60),
        cost_estimate=cost(),
        name="token_grads",
    )(select, back)


def exchange(x):
    experts = lax.axis_size("expert")
    y = lax.all_to_all(
        x.reshape(experts, ROWS, -1), "expert", split_axis=0, concat_axis=0, tiled=True
    )
    return y.reshape(x.shape)


def plane_exchange(x):
    count = lax.axis_size("expert") // PLANES
    groups = [[z * count + i for i in range(count)] for z in range(PLANES)]
    return lax.all_to_all(
        x, "expert", split_axis=0, concat_axis=0, tiled=True, axis_index_groups=groups
    )


def along(x, planes):
    experts = lax.axis_size("expert")
    count = experts // PLANES
    return lax.ppermute(
        x, "expert", [(i, (i + planes * count) % experts) for i in range(experts)]
    )


def swap(x):
    return lax.ppermute(x, "mp", [(0, 1), (1, 0)])


def body(tokens, cotangent, route_ids, gate_probs, w_gate, w_up, w_down):
    experts = lax.axis_size("expert")
    count = experts // PLANES
    plane = lax.axis_index("expert") // count
    mine = jnp.stack([lax.axis_index("mp"), plane]).astype(jnp.int32)
    first = (plane * count).astype(jnp.int32).reshape(1)
    route_t, probs_t = route_ids.T, gate_probs.T
    gate_w, up_w, down_w = w_gate[0], w_up[0], w_down[0]

    send_tokens = send_rows(route_t, tokens, experts)
    info = jnp.concatenate([route_t.astype(F32), probs_t], axis=0)
    infos = [info] + [along(info, r) for r in range(1, PLANES)]
    info = jnp.concatenate(infos, axis=1)
    cots = [cotangent] + [along(cotangent, r) for r in range(1, PLANES)]
    send_scaled = plane_send(first, info, cots, count)
    got_tokens, send_scaled = lax.optimization_barrier((exchange(send_tokens), send_scaled))
    got_scaled = plane_exchange(send_scaled)

    gate_pre, up_pre, hidden, token_rows, far0, far1, out_near = forward(
        mine, got_tokens, swap(got_tokens), gate_w, up_w, down_w
    )
    send_out = add_halves(out_near, [swap(far0), swap(far1)])
    got_scaled, send_out = lax.optimization_barrier((got_scaled, send_out))
    back_out = plane_exchange(send_out)

    other_scaled = swap(got_scaled)
    gate_grad, up_grad, far0, far1, in_near = backward(
        mine, got_scaled, other_scaled, gate_w, up_w, down_w, gate_pre, up_pre
    )
    send_in = pack(mine, in_near, [swap(far0), swap(far1)])
    back_out, send_in = lax.optimization_barrier((back_out, send_in))
    back_in = exchange(send_in)

    *parts, grad_part = token_outputs(first, info, cots, back_out)
    toks = tokens.shape[0]
    grad_parts = [grad_part[:, r * toks : (r + 1) * toks] for r in range(PLANES)]
    layer_out = parts[0].astype(F32)
    grad_probs = grad_parts[0]
    for r in range(1, PLANES):
        layer_out += along(parts[r], PLANES - r).astype(F32)
        grad_probs += along(grad_parts[r], PLANES - r)
    layer_out = layer_out.astype(BF16)
    grad_probs = lax.psum(grad_probs, "mp").T
    grad_w_gate, grad_w_up, grad_w_down = weight_grads(
        mine, token_rows, got_scaled, other_scaled, hidden, gate_grad, up_grad
    )
    grad_tokens = token_grads(select_rows(route_t, experts), back_in)
    return (
        layer_out, grad_tokens, grad_probs, grad_w_gate[None], grad_w_up[None], grad_w_down[None],
    )


def solution(mesh):
    return jax.shard_map(
        body,
        mesh=mesh,
        in_specs=(
            P("expert", "mp"),
            P("expert", "mp"),
            P("expert", None),
            P("expert", None),
            P("expert", None, "mp"),
            P("expert", None, "mp"),
            P("expert", "mp", None),
        ),
        out_specs=(
            P("expert", "mp"),
            P("expert", "mp"),
            P("expert", None),
            P("expert", None, "mp"),
            P("expert", None, "mp"),
            P("expert", "mp", None),
        ),
        check_vma=False,
    )
```

```python
import functools
import jax
import jax.numpy as jnp
from jax import lax
from jax.experimental import pallas as pl
from jax.experimental.pallas import tpu as pltpu
from jax.sharding import PartitionSpec as P

BF16 = jnp.bfloat16
F32 = jnp.float32
SLOTS = 12
ROWS = 2 * SLOTS
GROUP = 16
TILE = GROUP * ROWS

NN = (((1,), (0,)), ((), ()))
NT = (((1,), (1,)), ((), ()))
TN = (((0,), (0,)), ((), ()))


def dot(a, b, dims=NN):
    return lax.dot_general(a, b, dims, preferred_element_type=F32)


def params(mebibytes):
    return pltpu.CompilerParams(
        vmem_limit_bytes=mebibytes * 1024 * 1024, dimension_semantics=("arbitrary",)
    )


def cost():
    return pl.CostEstimate(flops=1, bytes_accessed=1, transcendentals=0)


def spread(rows_of):
    return jnp.concatenate(
        [jnp.broadcast_to(rows_of[i : i + 1], (ROWS, rows_of.shape[1])) for i in range(GROUP)], axis=0
    )


def routing(route_ref, first):
    top, toks = route_ref.shape
    route = route_ref[...]
    ids = lax.broadcasted_iota(jnp.int32, (GROUP, toks), 0) + first
    hits = [jnp.broadcast_to(route[k : k + 1], (GROUP, toks)) == ids for k in range(top)]
    named = sum(h.astype(F32) for h in hits)
    return named, hits


def selection(named):
    toks = named.shape[1]
    before = (
        lax.broadcasted_iota(jnp.int32, (toks, toks), 0)
        < lax.broadcasted_iota(jnp.int32, (toks, toks), 1)
    ).astype(BF16)
    slot = dot(named.astype(BF16), before)
    code = jnp.where(named > 0, slot, -100.0)
    code = jnp.concatenate([code, code + float(SLOTS)], axis=1)
    place = lax.broadcasted_iota(jnp.int32, (ROWS, 2 * toks), 0).astype(F32)
    place = jnp.concatenate([place] * GROUP, axis=0)
    return spread(code) == place


def probs_of(hits, probs_ref):
    probs = probs_ref[...]
    chosen = sum(
        jnp.where(h, jnp.broadcast_to(probs[k : k + 1], h.shape), 0.0) for k, h in enumerate(hits)
    )
    return spread(jnp.concatenate([chosen, chosen], axis=1))


def stacked(x):
    half = x.shape[1] // 2
    return jnp.concatenate([x[:, :half], x[:, half:]], axis=0)


def send_kernel(scaled, route_ref, probs_ref, rows_ref, out_ref):
    named, hits = routing(route_ref, pl.program_id(0) * GROUP)
    sel = selection(named)
    picked = dot(sel.astype(F32).astype(BF16), stacked(rows_ref[...]))
    if scaled:
        weight = jnp.sum(jnp.where(sel, probs_of(hits, probs_ref), 0.0), axis=1, keepdims=True)
        picked = picked * weight
    out_ref[...] = picked.astype(BF16)


def send_rows(scaled, route_t, probs_t, rows, experts):
    toks, width = rows.shape
    top = route_t.shape[0]
    half = width // 2
    return pl.pallas_call(
        functools.partial(send_kernel, scaled),
        grid=(experts // GROUP,),
        in_specs=[
            pl.BlockSpec((top, toks), lambda i: (0, 0)),
            pl.BlockSpec((top, toks), lambda i: (0, 0)),
            pl.BlockSpec((toks, width), lambda i: (0, 0)),
        ],
        out_specs=pl.BlockSpec((TILE, half), lambda i: (i, 0)),
        out_shape=jax.ShapeDtypeStruct((experts * ROWS, half), BF16),
        compiler_params=params(60),
        cost_estimate=cost(),
        name="send_scaled" if scaled else "send_tokens",
    )(route_t, probs_t, rows)


SUB = 8


def ordering(back=False):
    n = SUB * ROWS
    row = lax.broadcasted_iota(jnp.int32, (n, n), int(back))
    col = lax.broadcasted_iota(jnp.int32, (n, n), 1 - int(back))
    upper = (row >= n // 2).astype(jnp.int32)
    within = row - upper * (n // 2)
    source = (within * 43) >> 9
    return (col == SLOTS * source + SLOTS * upper + within).astype(F32).astype(BF16)


def put_in_order(own_ref, other_ref, mine, step, held, out_ref):
    order = ordering()
    n = SUB * ROWS
    quarter = own_ref.shape[1]
    for which, ref in ((mine, own_ref), (1 - mine, other_ref)):
        for b in range(own_ref.shape[0] // n):
            both = dot(order, ref[b * n : (b + 1) * n, :]).astype(BF16)
            row = pl.multiple_of((step * (own_ref.shape[0] // n) + b) * (n // 2), n // 2)
            for h in range(2):
                part = both[h * (n // 2) : (h + 1) * (n // 2)]
                lane = pl.multiple_of((2 * which + h) * quarter, quarter)
                held[pl.ds(row, n // 2), pl.ds(lane, quarter)] = part
                out_ref[b * (n // 2) : (b + 1) * (n // 2), pl.ds(lane, quarter)] = part


def weight_copies(gate_hbm, up_hbm, down_hbm, pair_w, down_w, sems):
    ff = down_w.shape[0]
    ins = [
        pltpu.make_async_copy(gate_hbm, pair_w.at[:, :ff], sems.at[0]),
        pltpu.make_async_copy(up_hbm, pair_w.at[:, ff:], sems.at[1]),
    ]
    return ins, [pltpu.make_async_copy(down_hbm, down_w, sems.at[2])]


def features(mine, half):
    return pl.ds(pl.multiple_of(mine * half, half), half)


def forward_kernel(
    steps, mine_ref, own_ref, other_ref, gate_hbm, up_hbm, down_hbm,
    gate_ref, up_ref, hidden_ref, rows_ref, far0, far1, near_ref, held, pair_w, down_w, sems,
):
    i = pl.program_id(0)
    mine = mine_ref[0]
    quarter = own_ref.shape[1]
    ff = down_w.shape[0]
    ins, downs = weight_copies(gate_hbm, up_hbm, down_hbm, pair_w, down_w, sems)

    @pl.when(i == 0)
    def _():
        for copy in ins + downs:
            copy.start()

    @pl.when(i < steps)
    def _():
        put_in_order(own_ref, other_ref, mine, i, held, rows_ref)

    @pl.when(i == steps)
    def _():
        for copy in ins:
            copy.wait()
        both = dot(held[...], pair_w[...])
        gate, up = both[:, :ff], both[:, ff:]
        gate_ref[...] = gate
        up_ref[...] = up
        hidden_ref[...] = (gate * jax.nn.sigmoid(gate) * up).astype(BF16)

    @pl.when(i == steps + 1)
    def _():
        for copy in downs:
            copy.wait()
        part = dot(hidden_ref[...], down_w[:, features(1 - mine, 2 * quarter)]).astype(BF16)
        far0[...] = part[:, :quarter]
        far1[...] = part[:, quarter:]

    @pl.when(i == steps + 2)
    def _():
        near_ref[...] = dot(hidden_ref[...], down_w[:, features(mine, 2 * quarter)]).astype(BF16)


A_TILE = 2 * TILE


def forward(mine, own, other, gate_w, up_w, down_w):
    raw, quarter = own.shape
    model, ff = gate_w.shape
    rows, steps = raw // 2, raw // A_TILE
    source = pl.BlockSpec((A_TILE, quarter), lambda i, m: (jnp.minimum(i, steps - 1), 0))
    ordered = pl.BlockSpec((A_TILE // 2, model), lambda i, m: (jnp.minimum(i, steps - 1), 0))
    whole = lambda width: pl.BlockSpec((rows, width), lambda i, m: (0, 0))
    hbm = pl.BlockSpec(memory_space=pl.ANY)
    return pl.pallas_call(
        functools.partial(forward_kernel, steps),
        grid_spec=pltpu.PrefetchScalarGridSpec(
            num_scalar_prefetch=1,
            grid=(steps + 3,),
            in_specs=[source, source, hbm, hbm, hbm],
            out_specs=[
                whole(ff), whole(ff), whole(ff), ordered, whole(quarter), whole(quarter),
                whole(2 * quarter),
            ],
            scratch_shapes=[
                pltpu.VMEM((rows, model), BF16),
                pltpu.VMEM((model, 2 * ff), BF16),
                pltpu.VMEM((ff, model), BF16),
                pltpu.SemaphoreType.DMA((3,)),
            ],
        ),
        out_shape=[
            jax.ShapeDtypeStruct((rows, ff), F32),
            jax.ShapeDtypeStruct((rows, ff), F32),
            jax.ShapeDtypeStruct((rows, ff), BF16),
            jax.ShapeDtypeStruct((rows, model), BF16),
            jax.ShapeDtypeStruct((rows, quarter), BF16),
            jax.ShapeDtypeStruct((rows, quarter), BF16),
            jax.ShapeDtypeStruct((rows, 2 * quarter), BF16),
        ],
        compiler_params=params(60),
        cost_estimate=cost(),
        name="expert_forward",
    )(mine, own, other, gate_w, up_w, down_w)


def backward_kernel(
    steps, mine_ref, own_ref, other_ref, gate_hbm, up_hbm, down_hbm, gate_ref, up_ref,
    grads_ref, rows_ref, far0, far1, near_ref, held, pair_w, down_w, sems,
):
    i = pl.program_id(0)
    mine = mine_ref[0]
    quarter = own_ref.shape[1]
    ff = down_w.shape[0]
    ins, downs = weight_copies(gate_hbm, up_hbm, down_hbm, pair_w, down_w, sems)

    @pl.when(i == 0)
    def _():
        for copy in downs + ins:
            copy.start()

    @pl.when(i < steps)
    def _():
        put_in_order(own_ref, other_ref, mine, i, held, rows_ref)

    @pl.when(i == steps)
    def _():
        for copy in downs:
            copy.wait()
        hidden_grad = dot(held[...], down_w[...], NT)
        gate, up = gate_ref[...], up_ref[...]
        logistic = jax.nn.sigmoid(gate)
        grads_ref[:, :ff] = (
            hidden_grad * up * logistic * (1.0 + gate * (1.0 - logistic))
        ).astype(BF16)
        grads_ref[:, ff:] = (hidden_grad * (gate * logistic)).astype(BF16)

    @pl.when(i == steps + 1)
    def _():
        for copy in ins:
            copy.wait()
        part = dot(grads_ref[...], pair_w[features(1 - mine, 2 * quarter), :], NT).astype(BF16)
        far0[...] = part[:, :quarter]
        far1[...] = part[:, quarter:]

    @pl.when(i == steps + 2)
    def _():
        near_ref[...] = dot(
            grads_ref[...], pair_w[features(mine, 2 * quarter), :], NT
        ).astype(BF16)


def backward(mine, own, other, gate_w, up_w, down_w, gate_pre, up_pre):
    raw, quarter = own.shape
    model, ff = gate_w.shape
    rows, steps = raw // 2, raw // A_TILE
    source = pl.BlockSpec((A_TILE, quarter), lambda i, m: (jnp.minimum(i, steps - 1), 0))
    ordered = pl.BlockSpec((A_TILE // 2, model), lambda i, m: (jnp.minimum(i, steps - 1), 0))
    whole = lambda width: pl.BlockSpec((rows, width), lambda i, m: (0, 0))
    hbm = pl.BlockSpec(memory_space=pl.ANY)
    return pl.pallas_call(
        functools.partial(backward_kernel, steps),
        grid_spec=pltpu.PrefetchScalarGridSpec(
            num_scalar_prefetch=1,
            grid=(steps + 3,),
            in_specs=[source, source, hbm, hbm, hbm, whole(ff), whole(ff)],
            out_specs=[
                whole(2 * ff), ordered, whole(quarter), whole(quarter), whole(2 * quarter)
            ],
            scratch_shapes=[
                pltpu.VMEM((rows, model), BF16),
                pltpu.VMEM((model, 2 * ff), BF16),
                pltpu.VMEM((ff, model), BF16),
                pltpu.SemaphoreType.DMA((3,)),
            ],
        ),
        out_shape=[
            jax.ShapeDtypeStruct((rows, 2 * ff), BF16),
            jax.ShapeDtypeStruct((rows, model), BF16),
            jax.ShapeDtypeStruct((rows, quarter), BF16),
            jax.ShapeDtypeStruct((rows, quarter), BF16),
            jax.ShapeDtypeStruct((rows, 2 * quarter), BF16),
        ],
        compiler_params=params(60),
        cost_estimate=cost(),
        name="expert_backward",
    )(mine, own, other, gate_w, up_w, down_w, gate_pre, up_pre)


def pack_kernel(near_ref, far0, far1, out_ref):
    order = ordering(back=True)
    n = SUB * ROWS
    quarter = out_ref.shape[1]
    for b in range(GROUP // SUB):
        at = slice(b * (n // 2), (b + 1) * (n // 2))
        both = jnp.concatenate(
            [
                (
                    near_ref[at, h * quarter : (h + 1) * quarter].astype(F32)
                    + far[at, :].astype(F32)
                ).astype(BF16)
                for h, far in enumerate((far0, far1))
            ],
            axis=0,
        )
        out_ref[b * n : (b + 1) * n, :] = dot(order, both).astype(BF16)


def pack(near, fars):
    rows, width = near.shape
    step_rows = GROUP * SLOTS
    return pl.pallas_call(
        pack_kernel,
        grid=(rows // step_rows,),
        in_specs=[
            pl.BlockSpec((step_rows, width), lambda i: (i, 0)),
            pl.BlockSpec((step_rows, width // 2), lambda i: (i, 0)),
            pl.BlockSpec((step_rows, width // 2), lambda i: (i, 0)),
        ],
        out_specs=pl.BlockSpec((TILE, width // 2), lambda i: (i, 0)),
        out_shape=jax.ShapeDtypeStruct((2 * rows, width // 2), BF16),
        compiler_params=params(48),
        cost_estimate=cost(),
        name="pack",
    )(near, *fars)


def weights_kernel(rows_ref, scaled_ref, hidden_ref, grads_ref, gate_w, up_w, down_w):
    ff = hidden_ref.shape[1]
    both = dot(rows_ref[...], grads_ref[...], TN)
    gate_w[...] = both[:, :ff].astype(BF16)
    up_w[...] = both[:, ff:].astype(BF16)
    down_w[...] = dot(hidden_ref[...], scaled_ref[...], TN).astype(BF16)


def weight_grads(token_rows, scaled_rows, hidden, grads):
    rows, model = token_rows.shape
    ff = hidden.shape[1]
    step = 512
    whole = lambda width: pl.BlockSpec((rows, width), lambda i: (0, 0))
    part = pl.BlockSpec((rows, step), lambda i: (0, i))
    return pl.pallas_call(
        weights_kernel,
        grid=(model // step,),
        in_specs=[part, part, whole(ff), whole(2 * ff)],
        out_specs=[
            pl.BlockSpec((step, ff), lambda i: (i, 0)),
            pl.BlockSpec((step, ff), lambda i: (i, 0)),
            pl.BlockSpec((ff, step), lambda i: (0, i)),
        ],
        out_shape=[
            jax.ShapeDtypeStruct((model, ff), BF16),
            jax.ShapeDtypeStruct((model, ff), BF16),
            jax.ShapeDtypeStruct((ff, model), BF16),
        ],
        compiler_params=params(60),
        cost_estimate=cost(),
        name="weight_grads",
    )(token_rows, scaled_rows, hidden, grads)


def outputs_kernel(route_ref, probs_ref, cot_ref, back_ref, out_ref, grad_ref, sel_ref, total):
    i = pl.program_id(0)

    @pl.when(i == 0)
    def _():
        total[...] = jnp.zeros_like(total)
        grad_ref[...] = jnp.zeros_like(grad_ref)

    toks = cot_ref.shape[0]
    half = back_ref.shape[1]
    named, hits = routing(route_ref, i * GROUP)
    sel = selection(named)
    sel_ref[...] = sel.astype(F32).T.astype(BF16)
    weight = jnp.where(sel, probs_of(hits, probs_ref), 0.0)
    high = weight.astype(BF16)
    low = (weight - high.astype(F32)).astype(BF16)
    back = back_ref[...]
    total[...] += dot(high, back, TN) + dot(low, back, TN)
    products = jnp.where(sel, dot(back, stacked(cot_ref[...]), NT), 0.0)
    sums = jnp.concatenate(
        [
            jnp.sum(products[e * ROWS : (e + 1) * ROWS], axis=0, keepdims=True)
            for e in range(GROUP)
        ],
        axis=0,
    )
    sums = sums[:, :toks] + sums[:, toks:]
    grad_ref[...] += jnp.concatenate(
        [jnp.sum(jnp.where(h, sums, 0.0), axis=0, keepdims=True) for h in hits], axis=0
    )

    @pl.when(i == pl.num_programs(0) - 1)
    def _():
        out_ref[:, :half] = total[:toks].astype(BF16)
        out_ref[:, half:] = total[toks:].astype(BF16)


def token_outputs(route_t, probs_t, cot, back):
    toks, width = cot.shape
    top = route_t.shape[0]
    steps = back.shape[0] // TILE
    small = pl.BlockSpec((top, toks), lambda i: (0, 0))
    wide = pl.BlockSpec((toks, width), lambda i: (0, 0))
    return pl.pallas_call(
        outputs_kernel,
        grid=(steps,),
        in_specs=[small, small, wide, pl.BlockSpec((TILE, width // 2), lambda i: (i, 0))],
        out_specs=[wide, small, pl.BlockSpec((2 * toks, TILE), lambda i: (0, i))],
        out_shape=[
            jax.ShapeDtypeStruct((toks, width), BF16),
            jax.ShapeDtypeStruct((top, toks), F32),
            jax.ShapeDtypeStruct((2 * toks, back.shape[0]), BF16),
        ],
        scratch_shapes=[pltpu.VMEM((2 * toks, width // 2), F32)],
        compiler_params=params(60),
        cost_estimate=cost(),
        name="token_outputs",
    )(route_t, probs_t, cot, back)


def inputs_kernel(sel_ref, back_ref, out_ref, total):
    i = pl.program_id(0)
    toks, width = out_ref.shape
    half = width // 2
    part = dot(sel_ref[...], back_ref[...])

    @pl.when(i == 0)
    def _():
        total[...] = part

    @pl.when(i > 0)
    def _():
        total[...] += part

    @pl.when(i == pl.num_programs(0) - 1)
    def _():
        out_ref[:, :half] = total[:toks].astype(BF16)
        out_ref[:, half:] = total[toks:].astype(BF16)


def token_grads(select, back):
    raw, half = back.shape
    toks = select.shape[0] // 2
    return pl.pallas_call(
        inputs_kernel,
        grid=(2,),
        in_specs=[
            pl.BlockSpec((2 * toks, raw // 2), lambda i: (0, i)),
            pl.BlockSpec((raw // 2, half), lambda i: (i, 0)),
        ],
        out_specs=pl.BlockSpec((toks, 2 * half), lambda i: (0, 0)),
        out_shape=jax.ShapeDtypeStruct((toks, 2 * half), BF16),
        scratch_shapes=[pltpu.VMEM((2 * toks, half), F32)],
        compiler_params=params(60),
        cost_estimate=cost(),
        name="token_grads",
    )(select, back)


def exchange(x):
    experts = lax.axis_size("expert")
    y = lax.all_to_all(
        x.reshape(experts, ROWS, -1), "expert", split_axis=0, concat_axis=0, tiled=True
    )
    return y.reshape(x.shape)


def swap(x):
    return lax.ppermute(x, "mp", [(0, 1), (1, 0)])


def body(tokens, cotangent, route_ids, gate_probs, w_gate, w_up, w_down):
    experts = lax.axis_size("expert")
    mine = lax.axis_index("mp").astype(jnp.int32).reshape(1)
    route_t, probs_t = route_ids.T, gate_probs.T
    gate_w, up_w, down_w = w_gate[0], w_up[0], w_down[0]

    send_tokens = send_rows(False, route_t, probs_t, tokens, experts)
    send_scaled = send_rows(True, route_t, probs_t, cotangent, experts)
    got_tokens, send_scaled = lax.optimization_barrier((exchange(send_tokens), send_scaled))
    got_scaled = exchange(send_scaled)

    gate_pre, up_pre, hidden, token_rows, far0, far1, out_near = forward(
        mine, got_tokens, swap(got_tokens), gate_w, up_w, down_w
    )
    send_out = pack(out_near, [swap(far0), swap(far1)])
    got_scaled, send_out = lax.optimization_barrier((got_scaled, send_out))
    back_out = exchange(send_out)

    grads, scaled_rows, far0, far1, in_near = backward(
        mine, got_scaled, swap(got_scaled), gate_w, up_w, down_w, gate_pre, up_pre
    )
    send_in = pack(in_near, [swap(far0), swap(far1)])
    back_out, send_in = lax.optimization_barrier((back_out, send_in))
    back_in = exchange(send_in)

    grad_w_gate, grad_w_up, grad_w_down = weight_grads(
        token_rows, scaled_rows, hidden, grads
    )
    layer_out, grad_part, select = token_outputs(route_t, probs_t, cotangent, back_out)
    grad_probs = lax.psum(grad_part, "mp").T
    grad_tokens = token_grads(select, back_in)
    return (
        layer_out, grad_tokens, grad_probs, grad_w_gate[None], grad_w_up[None], grad_w_down[None],
    )


def solution(mesh):
    return jax.shard_map(
        body,
        mesh=mesh,
        in_specs=(
            P("expert", "mp"),
            P("expert", "mp"),
            P("expert", None),
            P("expert", None),
            P("expert", None, "mp"),
            P("expert", None, "mp"),
            P("expert", "mp", None),
        ),
        out_specs=(
            P("expert", "mp"),
            P("expert", "mp"),
            P("expert", None),
            P("expert", None, "mp"),
            P("expert", None, "mp"),
            P("expert", "mp", None),
        ),
        check_vma=False,
    )
```

```python
import functools
import jax
import jax.numpy as jnp
from jax import lax
from jax.experimental import pallas as pl
from jax.experimental.pallas import tpu as pltpu
from jax.sharding import PartitionSpec as P

BF16 = jnp.bfloat16
F32 = jnp.float32
SLOTS = 12
ROWS = 2 * SLOTS
GROUP = 16
TILE = GROUP * ROWS

NN = (((1,), (0,)), ((), ()))
NT = (((1,), (1,)), ((), ()))
TN = (((0,), (0,)), ((), ()))


def dot(a, b, dims=NN):
    return lax.dot_general(a, b, dims, preferred_element_type=F32)


def params(mebibytes):
    return pltpu.CompilerParams(
        vmem_limit_bytes=mebibytes * 1024 * 1024, dimension_semantics=("arbitrary",)
    )


def cost():
    return pl.CostEstimate(flops=1, bytes_accessed=1, transcendentals=0)


def spread(rows_of):
    count, width = rows_of.shape
    return jnp.concatenate(
        [jnp.broadcast_to(rows_of[i : i + 1], (ROWS, width)) for i in range(count)], axis=0
    )


def routing(route_ref, first, count):
    top, toks = route_ref.shape
    route = route_ref[...]
    ids = lax.broadcasted_iota(jnp.int32, (count, toks), 0) + first
    hits = [jnp.broadcast_to(route[k : k + 1], (count, toks)) == ids for k in range(top)]
    named = sum(h.astype(F32) for h in hits)
    return named, hits


def selection(named):
    count, toks = named.shape
    before = (
        lax.broadcasted_iota(jnp.int32, (toks, toks), 0)
        < lax.broadcasted_iota(jnp.int32, (toks, toks), 1)
    ).astype(BF16)
    slot = dot(named.astype(BF16), before)
    code = jnp.where(named > 0, slot, -100.0)
    code = jnp.concatenate([code, code + float(SLOTS)], axis=1)
    place = lax.broadcasted_iota(jnp.int32, (ROWS, 2 * toks), 0).astype(F32)
    place = jnp.concatenate([place] * count, axis=0)
    return spread(code) == place


def probs_of(hits, probs_ref):
    probs = probs_ref[...]
    chosen = sum(
        jnp.where(h, jnp.broadcast_to(probs[k : k + 1], h.shape), 0.0) for k, h in enumerate(hits)
    )
    return spread(jnp.concatenate([chosen, chosen], axis=1))


def stacked(x):
    half = x.shape[1] // 2
    return jnp.concatenate([x[:, :half], x[:, half:]], axis=0)


def send_kernel(scaled, route_ref, probs_ref, rows_ref, out_ref):
    count = out_ref.shape[0] // ROWS
    named, hits = routing(route_ref, pl.program_id(0) * count, count)
    sel = selection(named)
    picked = dot(sel.astype(F32).astype(BF16), stacked(rows_ref[...]))
    if scaled:
        weight = jnp.sum(jnp.where(sel, probs_of(hits, probs_ref), 0.0), axis=1, keepdims=True)
        picked = picked * weight
    out_ref[...] = picked.astype(BF16)


SEND_STEP = 32


def send_rows(scaled, route_t, probs_t, rows, experts):
    toks, width = rows.shape
    top = route_t.shape[0]
    half = width // 2
    return pl.pallas_call(
        functools.partial(send_kernel, scaled),
        grid=(experts // SEND_STEP,),
        in_specs=[
            pl.BlockSpec((top, toks), lambda i: (0, 0)),
            pl.BlockSpec((top, toks), lambda i: (0, 0)),
            pl.BlockSpec((toks, width), lambda i: (0, 0)),
        ],
        out_specs=pl.BlockSpec((SEND_STEP * ROWS, half), lambda i: (i, 0)),
        out_shape=jax.ShapeDtypeStruct((experts * ROWS, half), BF16),
        compiler_params=params(52 if scaled else 60),
        cost_estimate=cost(),
        name="send_scaled" if scaled else "send_tokens",
    )(route_t, probs_t, rows)


SUB = 8


def ordering(back=False):
    n = SUB * ROWS
    row = lax.broadcasted_iota(jnp.int32, (n, n), int(back))
    col = lax.broadcasted_iota(jnp.int32, (n, n), 1 - int(back))
    upper = (row >= n // 2).astype(jnp.int32)
    within = row - upper * (n // 2)
    source = (within * 43) >> 9
    return (col == SLOTS * source + SLOTS * upper + within).astype(F32).astype(BF16)


def put_in_order(own_ref, other_ref, mine, step, held, out_ref):
    order = ordering()
    n = SUB * ROWS
    quarter = own_ref.shape[1]
    for which, ref in ((mine, own_ref), (1 - mine, other_ref)):
        for b in range(own_ref.shape[0] // n):
            both = dot(order, ref[b * n : (b + 1) * n, :]).astype(BF16)
            row = pl.multiple_of((step * (own_ref.shape[0] // n) + b) * (n // 2), n // 2)
            for h in range(2):
                part = both[h * (n // 2) : (h + 1) * (n // 2)]
                lane = pl.multiple_of((2 * which + h) * quarter, quarter)
                held[pl.ds(row, n // 2), pl.ds(lane, quarter)] = part
                out_ref[b * (n // 2) : (b + 1) * (n // 2), pl.ds(lane, quarter)] = part


def weight_copies(gate_hbm, up_hbm, down_hbm, pair_w, down_w, sems):
    ff = down_w.shape[0]
    ins = [
        pltpu.make_async_copy(gate_hbm, pair_w.at[:, :ff], sems.at[0]),
        pltpu.make_async_copy(up_hbm, pair_w.at[:, ff:], sems.at[1]),
    ]
    return ins, [pltpu.make_async_copy(down_hbm, down_w, sems.at[2])]


def features(mine, half):
    return pl.ds(pl.multiple_of(mine * half, half), half)


def forward_kernel(
    steps, mine_ref, own_ref, other_ref, gate_hbm, up_hbm, down_hbm,
    gate_ref, up_ref, hidden_ref, rows_ref, far0, far1, near_ref, held, pair_w, down_w, sems,
):
    i = pl.program_id(0)
    mine = mine_ref[0]
    quarter = own_ref.shape[1]
    ff = down_w.shape[0]
    ins, downs = weight_copies(gate_hbm, up_hbm, down_hbm, pair_w, down_w, sems)

    @pl.when(i == 0)
    def _():
        for copy in ins + downs:
            copy.start()

    @pl.when(i < steps)
    def _():
        put_in_order(own_ref, other_ref, mine, i, held, rows_ref)

    @pl.when(i == steps)
    def _():
        for copy in ins:
            copy.wait()
        both = dot(held[...], pair_w[...])
        gate, up = both[:, :ff], both[:, ff:]
        gate_ref[...] = gate
        up_ref[...] = up
        hidden_ref[...] = (gate * jax.nn.sigmoid(gate) * up).astype(BF16)

    @pl.when(i == steps + 1)
    def _():
        for copy in downs:
            copy.wait()
        part = dot(hidden_ref[...], down_w[:, features(1 - mine, 2 * quarter)]).astype(BF16)
        far0[...] = part[:, :quarter]
        far1[...] = part[:, quarter:]

    @pl.when(i == steps + 2)
    def _():
        near_ref[...] = dot(hidden_ref[...], down_w[:, features(mine, 2 * quarter)]).astype(BF16)


A_TILE = 2 * TILE


def forward(mine, own, other, gate_w, up_w, down_w):
    raw, quarter = own.shape
    model, ff = gate_w.shape
    rows, steps = raw // 2, raw // A_TILE
    source = pl.BlockSpec((A_TILE, quarter), lambda i, m: (jnp.minimum(i, steps - 1), 0))
    ordered = pl.BlockSpec((A_TILE // 2, model), lambda i, m: (jnp.minimum(i, steps - 1), 0))
    whole = lambda width: pl.BlockSpec((rows, width), lambda i, m: (0, 0))
    hbm = pl.BlockSpec(memory_space=pl.ANY)
    return pl.pallas_call(
        functools.partial(forward_kernel, steps),
        grid_spec=pltpu.PrefetchScalarGridSpec(
            num_scalar_prefetch=1,
            grid=(steps + 3,),
            in_specs=[source, source, hbm, hbm, hbm],
            out_specs=[
                whole(ff), whole(ff), whole(ff), ordered, whole(quarter), whole(quarter),
                whole(2 * quarter),
            ],
            scratch_shapes=[
                pltpu.VMEM((rows, model), BF16),
                pltpu.VMEM((model, 2 * ff), BF16),
                pltpu.VMEM((ff, model), BF16),
                pltpu.SemaphoreType.DMA((3,)),
            ],
        ),
        out_shape=[
            jax.ShapeDtypeStruct((rows, ff), F32),
            jax.ShapeDtypeStruct((rows, ff), F32),
            jax.ShapeDtypeStruct((rows, ff), BF16),
            jax.ShapeDtypeStruct((rows, model), BF16),
            jax.ShapeDtypeStruct((rows, quarter), BF16),
            jax.ShapeDtypeStruct((rows, quarter), BF16),
            jax.ShapeDtypeStruct((rows, 2 * quarter), BF16),
        ],
        compiler_params=params(60),
        cost_estimate=cost(),
        name="expert_forward",
    )(mine, own, other, gate_w, up_w, down_w)


def backward_kernel(
    steps, mine_ref, own_ref, other_ref, gate_hbm, up_hbm, down_hbm, gate_ref, up_ref,
    grads_ref, rows_ref, far0, far1, near_ref, held, pair_w, down_w, sems,
):
    i = pl.program_id(0)
    mine = mine_ref[0]
    quarter = own_ref.shape[1]
    ff = down_w.shape[0]
    ins, downs = weight_copies(gate_hbm, up_hbm, down_hbm, pair_w, down_w, sems)

    @pl.when(i == 0)
    def _():
        for copy in downs + ins:
            copy.start()

    @pl.when(i < steps)
    def _():
        put_in_order(own_ref, other_ref, mine, i, held, rows_ref)

    @pl.when(i == steps)
    def _():
        for copy in downs:
            copy.wait()
        hidden_grad = dot(held[...], down_w[...], NT)
        gate, up = gate_ref[...], up_ref[...]
        logistic = jax.nn.sigmoid(gate)
        grads_ref[:, :ff] = (
            hidden_grad * up * logistic * (1.0 + gate * (1.0 - logistic))
        ).astype(BF16)
        grads_ref[:, ff:] = (hidden_grad * (gate * logistic)).astype(BF16)

    @pl.when(i == steps + 1)
    def _():
        for copy in ins:
            copy.wait()
        part = dot(grads_ref[...], pair_w[features(1 - mine, 2 * quarter), :], NT).astype(BF16)
        far0[...] = part[:, :quarter]
        far1[...] = part[:, quarter:]

    @pl.when(i == steps + 2)
    def _():
        near_ref[...] = dot(
            grads_ref[...], pair_w[features(mine, 2 * quarter), :], NT
        ).astype(BF16)


def backward(mine, own, other, gate_w, up_w, down_w, gate_pre, up_pre):
    raw, quarter = own.shape
    model, ff = gate_w.shape
    rows, steps = raw // 2, raw // A_TILE
    source = pl.BlockSpec((A_TILE, quarter), lambda i, m: (jnp.minimum(i, steps - 1), 0))
    ordered = pl.BlockSpec((A_TILE // 2, model), lambda i, m: (jnp.minimum(i, steps - 1), 0))
    whole = lambda width: pl.BlockSpec((rows, width), lambda i, m: (0, 0))
    hbm = pl.BlockSpec(memory_space=pl.ANY)
    return pl.pallas_call(
        functools.partial(backward_kernel, steps),
        grid_spec=pltpu.PrefetchScalarGridSpec(
            num_scalar_prefetch=1,
            grid=(steps + 3,),
            in_specs=[source, source, hbm, hbm, hbm, whole(ff), whole(ff)],
            out_specs=[
                whole(2 * ff), ordered, whole(quarter), whole(quarter), whole(2 * quarter)
            ],
            scratch_shapes=[
                pltpu.VMEM((rows, model), BF16),
                pltpu.VMEM((model, 2 * ff), BF16),
                pltpu.VMEM((ff, model), BF16),
                pltpu.SemaphoreType.DMA((3,)),
            ],
        ),
        out_shape=[
            jax.ShapeDtypeStruct((rows, 2 * ff), BF16),
            jax.ShapeDtypeStruct((rows, model), BF16),
            jax.ShapeDtypeStruct((rows, quarter), BF16),
            jax.ShapeDtypeStruct((rows, quarter), BF16),
            jax.ShapeDtypeStruct((rows, 2 * quarter), BF16),
        ],
        compiler_params=params(60),
        cost_estimate=cost(),
        name="expert_backward",
    )(mine, own, other, gate_w, up_w, down_w, gate_pre, up_pre)


def pack_kernel(near_ref, far0, far1, out_ref):
    order = ordering(back=True)
    n = SUB * ROWS
    quarter = out_ref.shape[1]
    for b in range(GROUP // SUB):
        at = slice(b * (n // 2), (b + 1) * (n // 2))
        both = jnp.concatenate(
            [
                (
                    near_ref[at, h * quarter : (h + 1) * quarter].astype(F32)
                    + far[at, :].astype(F32)
                ).astype(BF16)
                for h, far in enumerate((far0, far1))
            ],
            axis=0,
        )
        out_ref[b * n : (b + 1) * n, :] = dot(order, both).astype(BF16)


def pack(near, fars):
    rows, width = near.shape
    step_rows = GROUP * SLOTS
    return pl.pallas_call(
        pack_kernel,
        grid=(rows // step_rows,),
        in_specs=[
            pl.BlockSpec((step_rows, width), lambda i: (i, 0)),
            pl.BlockSpec((step_rows, width // 2), lambda i: (i, 0)),
            pl.BlockSpec((step_rows, width // 2), lambda i: (i, 0)),
        ],
        out_specs=pl.BlockSpec((TILE, width // 2), lambda i: (i, 0)),
        out_shape=jax.ShapeDtypeStruct((2 * rows, width // 2), BF16),
        compiler_params=params(50),
        cost_estimate=cost(),
        name="pack",
    )(near, *fars)


def weights_kernel(rows_ref, scaled_ref, hidden_ref, grads_ref, gate_w, up_w, down_w):
    ff = hidden_ref.shape[1]
    both = dot(rows_ref[...], grads_ref[...], TN)
    gate_w[...] = both[:, :ff].astype(BF16)
    up_w[...] = both[:, ff:].astype(BF16)
    down_w[...] = dot(hidden_ref[...], scaled_ref[...], TN).astype(BF16)


def weight_grads(token_rows, scaled_rows, hidden, grads):
    rows, model = token_rows.shape
    ff = hidden.shape[1]
    step = 512
    whole = lambda width: pl.BlockSpec((rows, width), lambda i: (0, 0))
    part = pl.BlockSpec((rows, step), lambda i: (0, i))
    return pl.pallas_call(
        weights_kernel,
        grid=(model // step,),
        in_specs=[part, part, whole(ff), whole(2 * ff)],
        out_specs=[
            pl.BlockSpec((step, ff), lambda i: (i, 0)),
            pl.BlockSpec((step, ff), lambda i: (i, 0)),
            pl.BlockSpec((ff, step), lambda i: (0, i)),
        ],
        out_shape=[
            jax.ShapeDtypeStruct((model, ff), BF16),
            jax.ShapeDtypeStruct((model, ff), BF16),
            jax.ShapeDtypeStruct((ff, model), BF16),
        ],
        compiler_params=params(60),
        cost_estimate=cost(),
        name="weight_grads",
    )(token_rows, scaled_rows, hidden, grads)


def outputs_kernel(route_ref, probs_ref, cot_ref, back_ref, out_ref, grad_ref, sel_ref, total):
    i = pl.program_id(0)

    @pl.when(i == 0)
    def _():
        total[...] = jnp.zeros_like(total)
        grad_ref[...] = jnp.zeros_like(grad_ref)

    toks = cot_ref.shape[0]
    half = back_ref.shape[1]
    named, hits = routing(route_ref, i * GROUP, GROUP)
    sel = selection(named)
    sel_ref[...] = sel.astype(F32).T.astype(BF16)
    weight = jnp.where(sel, probs_of(hits, probs_ref), 0.0)
    high = weight.astype(BF16)
    low = (weight - high.astype(F32)).astype(BF16)
    back = back_ref[...]
    total[...] += dot(high, back, TN) + dot(low, back, TN)
    products = jnp.where(sel, dot(back, stacked(cot_ref[...]), NT), 0.0)
    sums = jnp.concatenate(
        [
            jnp.sum(products[e * ROWS : (e + 1) * ROWS], axis=0, keepdims=True)
            for e in range(GROUP)
        ],
        axis=0,
    )
    sums = sums[:, :toks] + sums[:, toks:]
    grad_ref[...] += jnp.concatenate(
        [jnp.sum(jnp.where(h, sums, 0.0), axis=0, keepdims=True) for h in hits], axis=0
    )

    @pl.when(i == pl.num_programs(0) - 1)
    def _():
        out_ref[:, :half] = total[:toks].astype(BF16)
        out_ref[:, half:] = total[toks:].astype(BF16)


def token_outputs(route_t, probs_t, cot, back):
    toks, width = cot.shape
    top = route_t.shape[0]
    steps = back.shape[0] // TILE
    small = pl.BlockSpec((top, toks), lambda i: (0, 0))
    wide = pl.BlockSpec((toks, width), lambda i: (0, 0))
    return pl.pallas_call(
        outputs_kernel,
        grid=(steps,),
        in_specs=[small, small, wide, pl.BlockSpec((TILE, width // 2), lambda i: (i, 0))],
        out_specs=[wide, small, pl.BlockSpec((2 * toks, TILE), lambda i: (0, i))],
        out_shape=[
            jax.ShapeDtypeStruct((toks, width), BF16),
            jax.ShapeDtypeStruct((top, toks), F32),
            jax.ShapeDtypeStruct((2 * toks, back.shape[0]), BF16),
        ],
        scratch_shapes=[pltpu.VMEM((2 * toks, width // 2), F32)],
        compiler_params=params(32),
        cost_estimate=cost(),
        name="token_outputs",
    )(route_t, probs_t, cot, back)


def inputs_kernel(sel_ref, back_ref, out_ref, total):
    i = pl.program_id(0)
    toks, width = out_ref.shape
    half = width // 2
    part = dot(sel_ref[...], back_ref[...])

    @pl.when(i == 0)
    def _():
        total[...] = part

    @pl.when(i > 0)
    def _():
        total[...] += part

    @pl.when(i == pl.num_programs(0) - 1)
    def _():
        out_ref[:, :half] = total[:toks].astype(BF16)
        out_ref[:, half:] = total[toks:].astype(BF16)


GRAD_STEPS = 2


def token_grads(select, back):
    raw, half = back.shape
    toks = select.shape[0] // 2
    return pl.pallas_call(
        inputs_kernel,
        grid=(GRAD_STEPS,),
        in_specs=[
            pl.BlockSpec((2 * toks, raw // GRAD_STEPS), lambda i: (0, i)),
            pl.BlockSpec((raw // GRAD_STEPS, half), lambda i: (i, 0)),
        ],
        out_specs=pl.BlockSpec((toks, 2 * half), lambda i: (0, 0)),
        out_shape=jax.ShapeDtypeStruct((toks, 2 * half), BF16),
        scratch_shapes=[pltpu.VMEM((2 * toks, half), F32)],
        compiler_params=params(60),
        cost_estimate=cost(),
        name="token_grads",
    )(select, back)


def exchange(x):
    experts = lax.axis_size("expert")
    y = lax.all_to_all(
        x.reshape(experts, ROWS, -1), "expert", split_axis=0, concat_axis=0, tiled=True
    )
    return y.reshape(x.shape)


def swap(x):
    return lax.ppermute(x, "mp", [(0, 1), (1, 0)])


def body(tokens, cotangent, route_ids, gate_probs, w_gate, w_up, w_down):
    experts = lax.axis_size("expert")
    mine = lax.axis_index("mp").astype(jnp.int32).reshape(1)
    route_t, probs_t = route_ids.T, gate_probs.T
    gate_w, up_w, down_w = w_gate[0], w_up[0], w_down[0]

    send_tokens = send_rows(False, route_t, probs_t, tokens, experts)
    send_scaled = send_rows(True, route_t, probs_t, cotangent, experts)
    got_tokens, send_scaled = lax.optimization_barrier((exchange(send_tokens), send_scaled))
    got_scaled = exchange(send_scaled)

    gate_pre, up_pre, hidden, token_rows, far0, far1, out_near = forward(
        mine, got_tokens, swap(got_tokens), gate_w, up_w, down_w
    )
    send_out = pack(out_near, [swap(far0), swap(far1)])
    got_scaled, send_out = lax.optimization_barrier((got_scaled, send_out))
    back_out = exchange(send_out)

    grads, scaled_rows, far0, far1, in_near = backward(
        mine, got_scaled, swap(got_scaled), gate_w, up_w, down_w, gate_pre, up_pre
    )
    send_in = pack(in_near, [swap(far0), swap(far1)])
    back_out, send_in = lax.optimization_barrier((back_out, send_in))
    back_in = exchange(send_in)

    layer_out, grad_part, select = token_outputs(route_t, probs_t, cotangent, back_out)
    grad_part, grads = lax.optimization_barrier((grad_part, grads))
    grad_w_gate, grad_w_up, grad_w_down = weight_grads(
        token_rows, scaled_rows, hidden, grads
    )
    grad_probs = lax.psum(grad_part, "mp").T
    grad_tokens = token_grads(select, back_in)
    return (
        layer_out, grad_tokens, grad_probs, grad_w_gate[None], grad_w_up[None], grad_w_down[None],
    )


def solution(mesh):
    return jax.shard_map(
        body,
        mesh=mesh,
        in_specs=(
            P("expert", "mp"),
            P("expert", "mp"),
            P("expert", None),
            P("expert", None),
            P("expert", None, "mp"),
            P("expert", None, "mp"),
            P("expert", "mp", None),
        ),
        out_specs=(
            P("expert", "mp"),
            P("expert", "mp"),
            P("expert", None),
            P("expert", None, "mp"),
            P("expert", None, "mp"),
            P("expert", "mp", None),
        ),
        check_vma=False,
    )
```

```python
import functools
import jax
import jax.numpy as jnp
from jax import lax
from jax.experimental import pallas as pl
from jax.experimental.pallas import tpu as pltpu
from jax.sharding import PartitionSpec as P

BF16 = jnp.bfloat16
F32 = jnp.float32
SLOTS = 12
ROWS = 2 * SLOTS
GROUP = 16
TILE = GROUP * ROWS

NN = (((1,), (0,)), ((), ()))
NT = (((1,), (1,)), ((), ()))
TN = (((0,), (0,)), ((), ()))


def dot(a, b, dims=NN):
    return lax.dot_general(a, b, dims, preferred_element_type=F32)


def params(mebibytes):
    return pltpu.CompilerParams(
        vmem_limit_bytes=mebibytes * 1024 * 1024, dimension_semantics=("arbitrary",)
    )


def cost():
    return pl.CostEstimate(flops=1, bytes_accessed=1, transcendentals=0)


def spread(rows_of):
    count, width = rows_of.shape
    return jnp.concatenate(
        [jnp.broadcast_to(rows_of[i : i + 1], (ROWS, width)) for i in range(count)], axis=0
    )


def routing(route_ref, first, count):
    top, toks = route_ref.shape
    route = route_ref[...]
    ids = lax.broadcasted_iota(jnp.int32, (count, toks), 0) + first
    hits = [jnp.broadcast_to(route[k : k + 1], (count, toks)) == ids for k in range(top)]
    named = sum(h.astype(F32) for h in hits)
    return named, hits


def selection(named):
    count, toks = named.shape
    before = (
        lax.broadcasted_iota(jnp.int32, (toks, toks), 0)
        < lax.broadcasted_iota(jnp.int32, (toks, toks), 1)
    ).astype(BF16)
    slot = dot(named.astype(BF16), before)
    code = jnp.where(named > 0, slot, -100.0)
    code = jnp.concatenate([code, code + float(SLOTS)], axis=1)
    place = lax.broadcasted_iota(jnp.int32, (ROWS, 2 * toks), 0).astype(F32)
    place = jnp.concatenate([place] * count, axis=0)
    return spread(code) == place


def probs_of(hits, probs_ref):
    probs = probs_ref[...]
    chosen = sum(
        jnp.where(h, jnp.broadcast_to(probs[k : k + 1], h.shape), 0.0) for k, h in enumerate(hits)
    )
    return spread(jnp.concatenate([chosen, chosen], axis=1))


def stacked(x):
    half = x.shape[1] // 2
    return jnp.concatenate([x[:, :half], x[:, half:]], axis=0)


def send_kernel(scaled, route_ref, probs_ref, rows_ref, out_ref):
    count = out_ref.shape[0] // ROWS
    named, hits = routing(route_ref, pl.program_id(0) * count, count)
    sel = selection(named)
    picked = dot(sel.astype(F32).astype(BF16), stacked(rows_ref[...]))
    if scaled:
        weight = jnp.sum(jnp.where(sel, probs_of(hits, probs_ref), 0.0), axis=1, keepdims=True)
        picked = picked * weight
    out_ref[...] = picked.astype(BF16)


SEND_STEP = 32


def send_rows(scaled, route_t, probs_t, rows, experts):
    toks, width = rows.shape
    top = route_t.shape[0]
    half = width // 2
    return pl.pallas_call(
        functools.partial(send_kernel, scaled),
        grid=(experts // SEND_STEP,),
        in_specs=[
            pl.BlockSpec((top, toks), lambda i: (0, 0)),
            pl.BlockSpec((top, toks), lambda i: (0, 0)),
            pl.BlockSpec((toks, width), lambda i: (0, 0)),
        ],
        out_specs=pl.BlockSpec((SEND_STEP * ROWS, half), lambda i: (i, 0)),
        out_shape=jax.ShapeDtypeStruct((experts * ROWS, half), BF16),
        compiler_params=params(52 if scaled else 60),
        cost_estimate=cost(),
        name="send_scaled" if scaled else "send_tokens",
    )(route_t, probs_t, rows)


SUB = 8


def ordering(back=False):
    n = SUB * ROWS
    row = lax.broadcasted_iota(jnp.int32, (n, n), int(back))
    col = lax.broadcasted_iota(jnp.int32, (n, n), 1 - int(back))
    upper = (row >= n // 2).astype(jnp.int32)
    within = row - upper * (n // 2)
    source = (within * 43) >> 9
    return (col == SLOTS * source + SLOTS * upper + within).astype(F32).astype(BF16)


def put_in_order(own_ref, other_ref, mine, step, held, out_ref):
    order = ordering()
    n = SUB * ROWS
    quarter = own_ref.shape[1]
    for which, ref in ((mine, own_ref), (1 - mine, other_ref)):
        for b in range(own_ref.shape[0] // n):
            both = dot(order, ref[b * n : (b + 1) * n, :]).astype(BF16)
            row = pl.multiple_of((step * (own_ref.shape[0] // n) + b) * (n // 2), n // 2)
            for h in range(2):
                part = both[h * (n // 2) : (h + 1) * (n // 2)]
                lane = pl.multiple_of((2 * which + h) * quarter, quarter)
                held[pl.ds(row, n // 2), pl.ds(lane, quarter)] = part
                out_ref[b * (n // 2) : (b + 1) * (n // 2), pl.ds(lane, quarter)] = part


def weight_copies(gate_hbm, up_hbm, down_hbm, pair_w, down_w, sems):
    ff = down_w.shape[0]
    ins = [
        pltpu.make_async_copy(gate_hbm, pair_w.at[:, :ff], sems.at[0]),
        pltpu.make_async_copy(up_hbm, pair_w.at[:, ff:], sems.at[1]),
    ]
    return ins, [pltpu.make_async_copy(down_hbm, down_w, sems.at[2])]


def features(mine, half):
    return pl.ds(pl.multiple_of(mine * half, half), half)


def forward_kernel(
    steps, mine_ref, own_ref, other_ref, gate_hbm, up_hbm, down_hbm,
    gate_ref, up_ref, hidden_ref, rows_ref, far0, far1, near_ref, held, pair_w, down_w, sems,
):
    i = pl.program_id(0)
    mine = mine_ref[0]
    quarter = own_ref.shape[1]
    ff = down_w.shape[0]
    ins, downs = weight_copies(gate_hbm, up_hbm, down_hbm, pair_w, down_w, sems)

    @pl.when(i == 0)
    def _():
        for copy in ins + downs:
            copy.start()

    @pl.when(i < steps)
    def _():
        put_in_order(own_ref, other_ref, mine, i, held, rows_ref)

    @pl.when(i == steps)
    def _():
        for copy in ins:
            copy.wait()
        both = dot(held[...], pair_w[...])
        gate, up = both[:, :ff], both[:, ff:]
        gate_ref[...] = gate
        up_ref[...] = up
        hidden_ref[...] = (gate * jax.nn.sigmoid(gate) * up).astype(BF16)

    @pl.when(i == steps + 1)
    def _():
        for copy in downs:
            copy.wait()
        part = dot(hidden_ref[...], down_w[:, features(1 - mine, 2 * quarter)]).astype(BF16)
        far0[...] = part[:, :quarter]
        far1[...] = part[:, quarter:]

    @pl.when(i == steps + 2)
    def _():
        near_ref[...] = dot(hidden_ref[...], down_w[:, features(mine, 2 * quarter)]).astype(BF16)


A_TILE = 2 * TILE


def forward(mine, own, other, gate_w, up_w, down_w):
    raw, quarter = own.shape
    model, ff = gate_w.shape
    rows, steps = raw // 2, raw // A_TILE
    source = pl.BlockSpec((A_TILE, quarter), lambda i, m: (jnp.minimum(i, steps - 1), 0))
    ordered = pl.BlockSpec((A_TILE // 2, model), lambda i, m: (jnp.minimum(i, steps - 1), 0))
    whole = lambda width: pl.BlockSpec((rows, width), lambda i, m: (0, 0))
    hbm = pl.BlockSpec(memory_space=pl.ANY)
    return pl.pallas_call(
        functools.partial(forward_kernel, steps),
        grid_spec=pltpu.PrefetchScalarGridSpec(
            num_scalar_prefetch=1,
            grid=(steps + 3,),
            in_specs=[source, source, hbm, hbm, hbm],
            out_specs=[
                whole(ff), whole(ff), whole(ff), ordered, whole(quarter), whole(quarter),
                whole(2 * quarter),
            ],
            scratch_shapes=[
                pltpu.VMEM((rows, model), BF16),
                pltpu.VMEM((model, 2 * ff), BF16),
                pltpu.VMEM((ff, model), BF16),
                pltpu.SemaphoreType.DMA((3,)),
            ],
        ),
        out_shape=[
            jax.ShapeDtypeStruct((rows, ff), F32),
            jax.ShapeDtypeStruct((rows, ff), F32),
            jax.ShapeDtypeStruct((rows, ff), BF16),
            jax.ShapeDtypeStruct((rows, model), BF16),
            jax.ShapeDtypeStruct((rows, quarter), BF16),
            jax.ShapeDtypeStruct((rows, quarter), BF16),
            jax.ShapeDtypeStruct((rows, 2 * quarter), BF16),
        ],
        compiler_params=params(60),
        cost_estimate=cost(),
        name="expert_forward",
    )(mine, own, other, gate_w, up_w, down_w)


def backward_kernel(
    steps, mine_ref, own_ref, other_ref, gate_hbm, up_hbm, down_hbm, gate_ref, up_ref,
    grads_ref, rows_ref, far0, far1, near_ref, held, pair_w, down_w, sems,
):
    i = pl.program_id(0)
    mine = mine_ref[0]
    quarter = own_ref.shape[1]
    ff = down_w.shape[0]
    ins, downs = weight_copies(gate_hbm, up_hbm, down_hbm, pair_w, down_w, sems)

    @pl.when(i == 0)
    def _():
        for copy in downs + ins:
            copy.start()

    @pl.when(i < steps)
    def _():
        put_in_order(own_ref, other_ref, mine, i, held, rows_ref)

    @pl.when(i == steps)
    def _():
        for copy in downs:
            copy.wait()
        hidden_grad = dot(held[...], down_w[...], NT)
        gate, up = gate_ref[...], up_ref[...]
        logistic = jax.nn.sigmoid(gate)
        grads_ref[:, :ff] = (
            hidden_grad * up * logistic * (1.0 + gate * (1.0 - logistic))
        ).astype(BF16)
        grads_ref[:, ff:] = (hidden_grad * (gate * logistic)).astype(BF16)

    @pl.when(i == steps + 1)
    def _():
        for copy in ins:
            copy.wait()
        part = dot(grads_ref[...], pair_w[features(1 - mine, 2 * quarter), :], NT).astype(BF16)
        far0[...] = part[:, :quarter]
        far1[...] = part[:, quarter:]

    @pl.when(i == steps + 2)
    def _():
        near_ref[...] = dot(
            grads_ref[...], pair_w[features(mine, 2 * quarter), :], NT
        ).astype(BF16)


def backward(mine, own, other, gate_w, up_w, down_w, gate_pre, up_pre):
    raw, quarter = own.shape
    model, ff = gate_w.shape
    rows, steps = raw // 2, raw // A_TILE
    source = pl.BlockSpec((A_TILE, quarter), lambda i, m: (jnp.minimum(i, steps - 1), 0))
    ordered = pl.BlockSpec((A_TILE // 2, model), lambda i, m: (jnp.minimum(i, steps - 1), 0))
    whole = lambda width: pl.BlockSpec((rows, width), lambda i, m: (0, 0))
    hbm = pl.BlockSpec(memory_space=pl.ANY)
    return pl.pallas_call(
        functools.partial(backward_kernel, steps),
        grid_spec=pltpu.PrefetchScalarGridSpec(
            num_scalar_prefetch=1,
            grid=(steps + 3,),
            in_specs=[source, source, hbm, hbm, hbm, whole(ff), whole(ff)],
            out_specs=[
                whole(2 * ff), ordered, whole(quarter), whole(quarter), whole(2 * quarter)
            ],
            scratch_shapes=[
                pltpu.VMEM((rows, model), BF16),
                pltpu.VMEM((model, 2 * ff), BF16),
                pltpu.VMEM((ff, model), BF16),
                pltpu.SemaphoreType.DMA((3,)),
            ],
        ),
        out_shape=[
            jax.ShapeDtypeStruct((rows, 2 * ff), BF16),
            jax.ShapeDtypeStruct((rows, model), BF16),
            jax.ShapeDtypeStruct((rows, quarter), BF16),
            jax.ShapeDtypeStruct((rows, quarter), BF16),
            jax.ShapeDtypeStruct((rows, 2 * quarter), BF16),
        ],
        compiler_params=params(60),
        cost_estimate=cost(),
        name="expert_backward",
    )(mine, own, other, gate_w, up_w, down_w, gate_pre, up_pre)


def pack_kernel(near_ref, far0, far1, out_ref):
    order = ordering(back=True)
    n = SUB * ROWS
    quarter = out_ref.shape[1]
    for b in range(GROUP // SUB):
        at = slice(b * (n // 2), (b + 1) * (n // 2))
        both = jnp.concatenate(
            [
                (
                    near_ref[at, h * quarter : (h + 1) * quarter].astype(F32)
                    + far[at, :].astype(F32)
                ).astype(BF16)
                for h, far in enumerate((far0, far1))
            ],
            axis=0,
        )
        out_ref[b * n : (b + 1) * n, :] = dot(order, both).astype(BF16)


def pack(near, fars):
    rows, width = near.shape
    step_rows = GROUP * SLOTS
    return pl.pallas_call(
        pack_kernel,
        grid=(rows // step_rows,),
        in_specs=[
            pl.BlockSpec((step_rows, width), lambda i: (i, 0)),
            pl.BlockSpec((step_rows, width // 2), lambda i: (i, 0)),
            pl.BlockSpec((step_rows, width // 2), lambda i: (i, 0)),
        ],
        out_specs=pl.BlockSpec((TILE, width // 2), lambda i: (i, 0)),
        out_shape=jax.ShapeDtypeStruct((2 * rows, width // 2), BF16),
        compiler_params=params(50),
        cost_estimate=cost(),
        name="pack",
    )(near, *fars)


def weights_kernel(rows_ref, scaled_ref, hidden_ref, grads_ref, gate_w, up_w, down_w):
    ff = hidden_ref.shape[1]
    both = dot(rows_ref[...], grads_ref[...], TN)
    gate_w[...] = both[:, :ff].astype(BF16)
    up_w[...] = both[:, ff:].astype(BF16)
    down_w[...] = dot(hidden_ref[...], scaled_ref[...], TN).astype(BF16)


def weight_grads(token_rows, scaled_rows, hidden, grads):
    rows, model = token_rows.shape
    ff = hidden.shape[1]
    step = 512
    whole = lambda width: pl.BlockSpec((rows, width), lambda i: (0, 0))
    part = pl.BlockSpec((rows, step), lambda i: (0, i))
    return pl.pallas_call(
        weights_kernel,
        grid=(model // step,),
        in_specs=[part, part, whole(ff), whole(2 * ff)],
        out_specs=[
            pl.BlockSpec((step, ff), lambda i: (i, 0)),
            pl.BlockSpec((step, ff), lambda i: (i, 0)),
            pl.BlockSpec((ff, step), lambda i: (0, i)),
        ],
        out_shape=[
            jax.ShapeDtypeStruct((model, ff), BF16),
            jax.ShapeDtypeStruct((model, ff), BF16),
            jax.ShapeDtypeStruct((ff, model), BF16),
        ],
        compiler_params=params(54),
        cost_estimate=cost(),
        name="weight_grads",
    )(token_rows, scaled_rows, hidden, grads)


def outputs_kernel(route_ref, probs_ref, cot_ref, back_ref, out_ref, grad_ref, sel_ref, total):
    i = pl.program_id(0)

    @pl.when(i == 0)
    def _():
        total[...] = jnp.zeros_like(total)
        grad_ref[...] = jnp.zeros_like(grad_ref)

    toks = cot_ref.shape[0]
    half = back_ref.shape[1]
    named, hits = routing(route_ref, i * GROUP, GROUP)
    sel = selection(named)
    sel_ref[...] = sel.astype(F32).T.astype(BF16)
    weight = jnp.where(sel, probs_of(hits, probs_ref), 0.0)
    high = weight.astype(BF16)
    low = (weight - high.astype(F32)).astype(BF16)
    back = back_ref[...]
    total[...] += dot(high, back, TN) + dot(low, back, TN)
    products = jnp.where(sel, dot(back, stacked(cot_ref[...]), NT), 0.0)
    sums = jnp.concatenate(
        [
            jnp.sum(products[e * ROWS : (e + 1) * ROWS], axis=0, keepdims=True)
            for e in range(GROUP)
        ],
        axis=0,
    )
    sums = sums[:, :toks] + sums[:, toks:]
    grad_ref[...] += jnp.concatenate(
        [jnp.sum(jnp.where(h, sums, 0.0), axis=0, keepdims=True) for h in hits], axis=0
    )

    @pl.when(i == pl.num_programs(0) - 1)
    def _():
        out_ref[:, :half] = total[:toks].astype(BF16)
        out_ref[:, half:] = total[toks:].astype(BF16)


def token_outputs(route_t, probs_t, cot, back):
    toks, width = cot.shape
    top = route_t.shape[0]
    steps = back.shape[0] // TILE
    small = pl.BlockSpec((top, toks), lambda i: (0, 0))
    wide = pl.BlockSpec((toks, width), lambda i: (0, 0))
    return pl.pallas_call(
        outputs_kernel,
        grid=(steps,),
        in_specs=[small, small, wide, pl.BlockSpec((TILE, width // 2), lambda i: (i, 0))],
        out_specs=[wide, small, pl.BlockSpec((2 * toks, TILE), lambda i: (0, i))],
        out_shape=[
            jax.ShapeDtypeStruct((toks, width), BF16),
            jax.ShapeDtypeStruct((top, toks), F32),
            jax.ShapeDtypeStruct((2 * toks, back.shape[0]), BF16),
        ],
        scratch_shapes=[pltpu.VMEM((2 * toks, width // 2), F32)],
        compiler_params=params(32),
        cost_estimate=cost(),
        name="token_outputs",
    )(route_t, probs_t, cot, back)


def inputs_kernel(sel_ref, back_ref, out_ref, total):
    i = pl.program_id(0)
    toks, width = out_ref.shape
    half = width // 2
    part = dot(sel_ref[...], back_ref[...])

    @pl.when(i == 0)
    def _():
        total[...] = part

    @pl.when(i > 0)
    def _():
        total[...] += part

    @pl.when(i == pl.num_programs(0) - 1)
    def _():
        out_ref[:, :half] = total[:toks].astype(BF16)
        out_ref[:, half:] = total[toks:].astype(BF16)


GRAD_STEPS = 2


def token_grads(select, back):
    raw, half = back.shape
    toks = select.shape[0] // 2
    return pl.pallas_call(
        inputs_kernel,
        grid=(GRAD_STEPS,),
        in_specs=[
            pl.BlockSpec((2 * toks, raw // GRAD_STEPS), lambda i: (0, i)),
            pl.BlockSpec((raw // GRAD_STEPS, half), lambda i: (i, 0)),
        ],
        out_specs=pl.BlockSpec((toks, 2 * half), lambda i: (0, 0)),
        out_shape=jax.ShapeDtypeStruct((toks, 2 * half), BF16),
        scratch_shapes=[pltpu.VMEM((2 * toks, half), F32)],
        compiler_params=params(16),
        cost_estimate=cost(),
        name="token_grads",
    )(select, back)


def exchange(x):
    experts = lax.axis_size("expert")
    y = lax.all_to_all(
        x.reshape(experts, ROWS, -1), "expert", split_axis=0, concat_axis=0, tiled=True
    )
    return y.reshape(x.shape)


def swap(x):
    return lax.ppermute(x, "mp", [(0, 1), (1, 0)])


def body(tokens, cotangent, route_ids, gate_probs, w_gate, w_up, w_down):
    experts = lax.axis_size("expert")
    mine = lax.axis_index("mp").astype(jnp.int32).reshape(1)
    route_t, probs_t = route_ids.T, gate_probs.T
    gate_w, up_w, down_w = w_gate[0], w_up[0], w_down[0]

    send_tokens = send_rows(False, route_t, probs_t, tokens, experts)
    send_scaled = send_rows(True, route_t, probs_t, cotangent, experts)
    got_tokens, send_scaled = lax.optimization_barrier((exchange(send_tokens), send_scaled))
    got_scaled = exchange(send_scaled)

    gate_pre, up_pre, hidden, token_rows, far0, far1, out_near = forward(
        mine, got_tokens, swap(got_tokens), gate_w, up_w, down_w
    )
    send_out = pack(out_near, [swap(far0), swap(far1)])
    got_scaled, send_out = lax.optimization_barrier((got_scaled, send_out))
    back_out = exchange(send_out)

    grads, scaled_rows, far0, far1, in_near = backward(
        mine, got_scaled, swap(got_scaled), gate_w, up_w, down_w, gate_pre, up_pre
    )
    send_in = pack(in_near, [swap(far0), swap(far1)])
    back_out, send_in = lax.optimization_barrier((back_out, send_in))
    back_in = exchange(send_in)

    layer_out, grad_part, select = token_outputs(route_t, probs_t, cotangent, back_out)
    grad_part, grads = lax.optimization_barrier((grad_part, grads))
    grad_w_gate, grad_w_up, grad_w_down = weight_grads(
        token_rows, scaled_rows, hidden, grads
    )
    grad_probs = lax.psum(grad_part, "mp").T
    grad_tokens = token_grads(select, back_in)
    return (
        layer_out, grad_tokens, grad_probs, grad_w_gate[None], grad_w_up[None], grad_w_down[None],
    )


def solution(mesh):
    return jax.shard_map(
        body,
        mesh=mesh,
        in_specs=(
            P("expert", "mp"),
            P("expert", "mp"),
            P("expert", None),
            P("expert", None),
            P("expert", None, "mp"),
            P("expert", None, "mp"),
            P("expert", "mp", None),
        ),
        out_specs=(
            P("expert", "mp"),
            P("expert", "mp"),
            P("expert", None),
            P("expert", None, "mp"),
            P("expert", None, "mp"),
            P("expert", "mp", None),
        ),
        check_vma=False,
    )
```
